32 devices in a mesh: dp: 2 (over y), owner: 4 (over z), context: 4 (over x, core).
Axes of the slice: x: 2, y: 2, z: 4, core: 2. Of those that a mesh axis runs over, the one named last changes fastest.
Arguments:
- grad_partials: bfloat16 [8, 1536, 32, 192], P(('dp', 'context'), None, 'owner')
- assignment: int32 [32, 1], replicated, may hold values from 0 to 3; in each aligned block of 8 rows (0 to 7, 8 to 15, ...) at most 2 rows name the same one
- momentum: float32 [32, 1536, 192], P('owner', ('dp', 'context')), may hold values from -6 to 6
- q_weight: float32 [32, 1536, 192], P('owner', ('dp', 'context')), may hold values from -1.2 to 1.2
- k_weight: float32 [32, 512, 128], P('owner', ('dp', 'context')), may hold values from -6 to 6
- max_logits: float32 [4, 32], P('context'), may hold values from 20 to 400
Outputs:
- momentum_out: float32 [32, 1536, 192], P('owner', ('dp', 'context'))
- q_weight_out: float32 [32, 1536, 192], P('owner', ('dp', 'context'))
- k_weight_out: float32 [32, 512, 128], P('owner', ('dp', 'context'))
The draws below stay inside these ranges and needn't reach their ends.
Inputs may be any that keep to these rules, and one draw needn't show every extreme that they name: `assignment`: in each aligned block of 8 heads no owner index is named more than 2 times, and some owner index exactly 2 times.
All inputs are finite; a program needn't handle non-finite values.
Results may differ from the reference program's by a relative error of at most 0.0007.
Values may be sent and summed in bfloat16 or wider, within the bound.
No kernel may reach another device: no remote copies, remote signals or barrier semaphores. Data moves between devices by JAX's collectives and lax.ppermute only.
A program may use at most 128 MiB of HBM per device.

```python
import math
import jax
import jax.numpy as jnp
import numpy as np
from jax import lax

QR = 1536
QK = 192
KN = 128
KVR = 512
HEADS_OWN = 8
C_SEND = 2
ITERS = 2
HEADS = 32
SLOTS_OWN = 8
SLOTS = 32
GRAD_PARTS = 8
LOGIT_PARTS = 4
N_OWNER = 4


def draw_grad_partials(key, part):
    key_noise = jax.random.fold_in(key, 11)
    key_rows = jax.random.fold_in(key, 12)
    key_columns = jax.random.fold_in(key, 13)
    key_left = jax.random.fold_in(key, 15)
    key_right = jax.random.fold_in(key, 16)
    row_top = 10.0
    factor_weight = 0.8
    row_scale = jnp.exp(jax.random.uniform(key_rows, (1, QR, 1, 1), jnp.float32, 0.0, math.log(row_top)))
    column_scale = jnp.exp(jax.random.uniform(key_columns, (1, 1, 1, QK), jnp.float32, 0.0, math.log(10.0)))
    block_rows = QR // GRAD_PARTS
    half_blocks = max(GRAD_PARTS // 2, 1)
    row_block = jnp.arange(QR, dtype=jnp.int32) // block_rows
    pair_index = row_block % half_blocks
    head_index = jnp.arange(HEADS, dtype=jnp.int32)
    column_target = (pair_index[:, None] * 5 + head_index[None, :] * 3) % QK
    column_index = jnp.arange(QK, dtype=jnp.int32)
    marked = (column_target[:, :, None] == column_index[None, None, :]).astype(jnp.float32)[None]
    boost = 1.0 + 5.0 * marked
    left_factor = jax.random.normal(key_left, (3, QR, HEADS), jnp.float32)
    right_factor = jax.random.normal(key_right, (3, HEADS, QK), jnp.float32)
    coupled = left_factor[0][:, :, None] * right_factor[0][None, :, :]
    coupled = coupled + left_factor[1][:, :, None] * right_factor[1][None, :, :]
    coupled = coupled + left_factor[2][:, :, None] * right_factor[2][None, :, :]
    coupled = coupled[None] * (factor_weight / GRAD_PARTS)
    values = jax.random.normal(key_noise, (GRAD_PARTS, QR, HEADS, QK), jnp.float32) / math.sqrt(GRAD_PARTS)
    return ((values + coupled) * boost * row_scale * column_scale * 0.07).astype(jnp.bfloat16)


def steps_of(stream_key, shape, cuts, low, largest):
    level, own = 1.0, jax.random.fold_in(stream_key, 6)
    for axis_at, parts in cuts:
        heights = jnp.exp(jax.random.uniform(jax.random.fold_in(own, axis_at), (parts,), jnp.float32, low / len(cuts), largest / len(cuts)))
        level = level * jnp.repeat(heights, shape[axis_at] // parts).reshape([-1 if axis == axis_at else 1 for axis in range(len(shape))])
    return level


def shared_out(rng, own, number, rows, number_of, top, bound, slope):
    ranking = jax.random.permutation(rng, number_of)
    packed, common = portions_of(number_of, rows * top, bound, slope, True), portions_of(number_of, rows * top, bound, slope, False)
    places = jnp.arange(number_of)

    def named(sizes, rotation):
        used = int((sizes > 0).sum())
        fixed = max(1, used // 4)
        moved = fixed + (places - fixed + rotation * (used - fixed)) % max(1, number_of - fixed)
        return jnp.zeros((number_of,), jnp.int32).at[ranking[jnp.where(places < fixed, places, moved)]].set(jnp.asarray(sizes, jnp.int32))

    sizes = jnp.where(number % 4 == 0, named(packed, number // 4), named(common, number - number // 4 - 1))
    mixed = jax.random.permutation(jax.random.fold_in(own, 3), number_of)
    source_of, receiver = mixed[0:number_of // 2 * 2:2], mixed[1:number_of // 2 * 2:2]
    slack = jnp.minimum(sizes[source_of] - 1, bound - sizes[receiver]) // 2
    slack = jnp.where((source_of == ranking[0]) | (receiver == ranking[0]) | (sizes[receiver] == 0), 0, jnp.maximum(slack, 0))
    moved = jax.random.randint(jax.random.fold_in(own, 4), (number_of // 2,), 0, 1 << 20) % (slack + 1)
    sizes = sizes.at[source_of].add(-moved).at[receiver].add(moved)
    items = jnp.searchsorted(jnp.cumsum(sizes), jnp.arange(rows * top), side="right").astype(jnp.int32)
    table = items.reshape(top, rows).T
    table = table[jax.random.permutation(jax.random.fold_in(own, 1), rows)]
    rotation = jax.random.randint(jax.random.fold_in(own, 2), (rows, 1), 0, top)
    return jnp.take_along_axis(table, (jnp.arange(top)[None, :] + rotation) % top, axis=1)


def portions_of(amount, total, bound, slope, full):
    loads = [(1 << 20) // math.isqrt(grade ** slope) + 1 for grade in range(1, amount + 1)]
    largest = bound if full else min(bound, max(-(-total // amount), total * loads[0] // sum(loads)))
    least = 1 if total - largest >= amount - 1 else 0
    holding, spare = [largest] + [least] * (amount - 1), total - largest - least * (amount - 1)
    while spare > 0:
        candidates = [i for i in range(1, amount) if holding[i] < largest] or [i for i in range(1, amount) if holding[i] < bound]
        pool, budget = sum([loads[i] for i in candidates]), spare
        for i in candidates:
            more = min(bound - holding[i], max(1, budget * loads[i] // pool), spare)
            holding[i] = holding[i] + more
            spare = spare - more
    return np.array(holding)


def centred(stream_key, shape, width, most, split=(), kind=jnp.bfloat16):
    drawn = jax.random.normal(stream_key, shape, jnp.float32) * width
    if len(split) > 0:
        drawn = steps_of(stream_key, shape, split, -0.22, 0.18) * drawn
    return jnp.clip(drawn, min=-most, max=most).astype(kind)


def setup_inputs(seed: int = 0) -> dict:
    key_of = jax.random.split(jax.random.key(seed), 7)
    grad_partials = draw_grad_partials(jax.random.fold_in(key_of[6], 71), 0)
    assignment_keys = jax.random.split(jax.random.fold_in(key_of[1], 1), HEADS // HEADS_OWN)
    assignment_turns = jax.random.permutation(jax.random.fold_in(key_of[1], 3), HEADS // HEADS_OWN)
    assignment = jax.vmap(lambda own, number: shared_out(jax.random.fold_in(key_of[1], 2), own, number, HEADS_OWN, N_OWNER, 1, C_SEND, 2))(assignment_keys, assignment_turns).reshape((HEADS, 1))
    momentum = centred(key_of[2], (SLOTS, QR, QK), 1.0, 6.0, ((0, 4), (1, 8)), jnp.float32)
    q_weight = centred(key_of[3], (SLOTS, QR, QK), 0.2, 1.2, ((0, 4), (1, 8)), jnp.float32)
    k_weight = centred(key_of[4], (HEADS, KVR, KN), 1.0, 6.0, ((0, 4), (1, 8)), jnp.float32)
    max_logits = jnp.clip(jnp.exp(math.log(400.0) - 2.9957323 * jax.random.uniform(key_of[5], (LOGIT_PARTS, HEADS), jnp.float32) ** steps_of(key_of[5], (LOGIT_PARTS, HEADS), ((0, 4),), -0.2, 0.2)), 20.0, 400.0)
    return dict(grad_partials=grad_partials, assignment=assignment, momentum=momentum, q_weight=q_weight, k_weight=k_weight, max_logits=max_logits)


MOMENTUM_RATE = 0.95
WEIGHT_KEEP = 0.98
LOGIT_CAP = 100.0
QUINTIC_A = 3.4445
QUINTIC_B = -4.775
QUINTIC_C = 2.0315

def routing(assignment, heads_own, per_source):
    target = assignment[:, 0]
    head_index = jnp.arange(target.shape[0], dtype=jnp.int32)
    source_block = head_index // heads_own
    earlier = (source_block[None, :] == source_block[:, None]) & (head_index[None, :] < head_index[:, None]) & (target[None, :] == target[:, None])
    position = lax.optimization_barrier(jnp.sum(earlier.astype(jnp.int32), axis=1)).astype(jnp.int32)
    return (target, position, (source_block * per_source + position).astype(jnp.int32))

def newton(matrix):
    square_sum = jnp.sum(matrix * matrix)
    iterate = (matrix / (jnp.sqrt(square_sum) + 1e-07)).astype(jnp.bfloat16)
    for step in range(ITERS):
        gram_matrix = jnp.dot(iterate.T, iterate, preferred_element_type=jnp.float32)
        polynomial = (QUINTIC_B * gram_matrix + QUINTIC_C * jnp.dot(gram_matrix, gram_matrix, precision=lax.Precision.HIGHEST)).astype(jnp.bfloat16)
        iterate = (QUINTIC_A * iterate.astype(jnp.float32) + jnp.dot(iterate, polynomial, preferred_element_type=jnp.float32)).astype(jnp.bfloat16)
    return iterate

def refresh(weight, orthogonal, gamma, kn_count):
    step_size = 0.04 * math.sqrt(max(QR, QK))
    column_index = jnp.arange(weight.shape[2])
    column_scale = jnp.where(column_index[None, :] < kn_count, jnp.sqrt(gamma)[:, None], gamma[:, None])
    return (WEIGHT_KEEP * weight - step_size * orthogonal.astype(jnp.float32)) * column_scale[:, None, :]

def reference(grad_partials, assignment, momentum, q_weight, k_weight, max_logits):

    def add_part(part_index, running):
        return running + lax.dynamic_index_in_dim(grad_partials, part_index, 0, keepdims=False).astype(jnp.float32)
    grad = lax.fori_loop(0, GRAD_PARTS, add_part, jnp.zeros((QR, HEADS, QK), jnp.float32))
    target, position, local_slot = routing(assignment, HEADS_OWN, C_SEND)
    slot = (target * SLOTS_OWN + local_slot).astype(jnp.int32)
    refreshed = MOMENTUM_RATE * momentum[slot] + jnp.transpose(grad, (1, 0, 2))
    momentum_out = momentum.at[slot].set(refreshed)
    orthogonal = lax.map(newton, refreshed)
    peak_logit = lax.optimization_barrier(jnp.max(max_logits, axis=0))
    gamma = jnp.minimum(1.0, LOGIT_CAP / peak_logit)
    q_weight_out = q_weight.at[slot].set(refresh(q_weight[slot], orthogonal, gamma, KN))
    k_weight_out = k_weight * jnp.sqrt(gamma)[:, None, None]
    return (momentum_out, q_weight_out, k_weight_out)
```

```python
import functools
import math

import jax
import jax.numpy as jnp
from jax import lax
from jax.experimental import pallas as pl
from jax.experimental.pallas import tpu as pltpu
from jax.sharding import PartitionSpec as P

ITERS = 2
MOMENTUM_RATE = 0.95
WEIGHT_KEEP = 0.98
LOGIT_CAP = 100.0
QUINTIC_A = 3.4445
QUINTIC_B = -4.775
QUINTIC_C = 2.0315

CORES = 2
PLANE = ("dp", "context")
SCALE_ROWS = 16
LEVELS = 14.99
STEPS = 8.0
CHUNKS = 2

SMEM = pl.BlockSpec(memory_space=pltpu.SMEM)
VMEM = pl.BlockSpec(memory_space=pltpu.VMEM)
PARAMS = pltpu.CompilerParams(vmem_limit_bytes=48 * 1024 * 1024)


def encode(values, out):
    top = jnp.max(jnp.abs(values), axis=0, keepdims=True)
    level = jnp.clip(jnp.ceil(STEPS * jnp.log2(top)), -100.0 * STEPS, 128.0 * STEPS)
    scaled = values * jnp.exp2(LEVELS - level * (1.0 / STEPS))
    count = values.shape[0]
    out[:count] = jnp.round(scaled).astype(jnp.int32).astype(jnp.int16)
    rows = jnp.broadcast_to(level, (SCALE_ROWS, values.shape[1]))
    out[count:] = rows.astype(jnp.int32).astype(jnp.int16)


def decode(block):
    count = block.shape[0] - SCALE_ROWS
    level = block[count : count + SCALE_ROWS].astype(jnp.int32).astype(jnp.float32)[0:1]
    return block[:count].astype(jnp.int32).astype(jnp.float32) * jnp.exp2(
        level * (1.0 / STEPS) - LEVELS
    )


def pair_kernel(chips, aligned, index, own, sibling, here, *away):
    width = here.shape[-1]
    for k in range(chips):
        chip = index[0] ^ k
        if aligned:
            rows = pl.ds(pl.multiple_of(chip * width, 128), width)
            first, second = own[0, :, rows], sibling[0, :, rows]
        else:
            first, second = own[0, chip], sibling[0, chip]
        total = first.astype(jnp.float32) + second.astype(jnp.float32)
        if k == 0:
            here[0] = total
        else:
            encode(total, away[k - 1].at[0])


def pair_sums(g, sibling, heads, chip, chips):
    count, cols = sibling.shape[0], sibling.shape[1 if sibling.ndim == 3 else 2]
    aligned = sibling.ndim == 3
    width = sibling.shape[2] // chips if aligned else sibling.shape[3]
    block = (1,) + sibling.shape[1:]
    zeros = (0,) * (sibling.ndim - 1)
    coded = jax.ShapeDtypeStruct((count, cols + SCALE_ROWS, width), jnp.int16)
    return pl.pallas_call(
        functools.partial(pair_kernel, chips, aligned),
        grid_spec=pltpu.PrefetchScalarGridSpec(
            num_scalar_prefetch=1,
            grid=(count,),
            in_specs=[
                pl.BlockSpec(block, lambda i, index: (index[i + 1],) + zeros),
                pl.BlockSpec(block, lambda i, index: (i,) + zeros),
            ],
            out_specs=[pl.BlockSpec((1, cols, width), lambda i, index: (i, 0, 0))]
            + [pl.BlockSpec((1, cols + SCALE_ROWS, width), lambda i, index: (i, 0, 0))]
            * (chips - 1),
        ),
        out_shape=[jax.ShapeDtypeStruct((count, cols, width), jnp.float32)] + [coded] * (chips - 1),
        compiler_params=PARAMS,
        name="pair_sum",
    )(jnp.concatenate([chip[None], heads]).astype(jnp.int32), g, sibling)


def plane_kernel(plain, here, *refs):
    count = here.shape[0]
    away, outs = refs[: len(refs) - count], refs[len(refs) - count :]
    for i in range(count):
        total = here[i]
        for block in away:
            total = total + decode(block[i])
        if plain[i]:
            outs[i][...] = total
        else:
            encode(total, outs[i])


def plane_sums(here, away, plain):
    count, cols, width = here.shape
    coded = jax.ShapeDtypeStruct((cols + SCALE_ROWS, width), jnp.int16)
    whole = jax.ShapeDtypeStruct((cols, width), jnp.float32)
    return pl.pallas_call(
        functools.partial(plane_kernel, plain),
        in_specs=[VMEM] * (1 + len(away)),
        out_specs=[VMEM] * count,
        out_shape=[whole if p else coded for p in plain],
        compiler_params=PARAMS,
        name="plane_sum",
    )(here, *away)


def turn_kernel(index, own, sibling, out, both):
    core = index[0]
    rows = own.shape[1]
    for s in range(sibling.shape[0]):
        both[pl.ds(pl.multiple_of(core * rows, 16), rows)] = own[s * CORES + core]
        both[pl.ds(pl.multiple_of((1 - core) * rows, 16), rows)] = sibling[s]
        out[s] = both[...].T


def turn(index, own, sibling):
    sources, rows, cols = sibling.shape
    return pl.pallas_call(
        turn_kernel,
        in_specs=[SMEM, VMEM, VMEM],
        out_specs=VMEM,
        out_shape=jax.ShapeDtypeStruct((sources, cols, CORES * rows), jnp.float32),
        scratch_shapes=[pltpu.VMEM((CORES * rows, cols), jnp.float32)],
        compiler_params=PARAMS,
        name="turn_momentum",
    )(index, own, sibling)


def refresh_kernel(chips, index, occupied, old, near, *refs):
    sources = old.shape[0]
    arrived, (new, here), away = refs[: sources - 1], refs[sources - 1 : sources + 1], refs[sources + 1 :]
    core, chip, owner = index[0], index[1], index[2]
    for k in range(sources):
        source = owner ^ k
        grad = near[...] if k == 0 else decode(arrived[k - 1])
        kept = old[source]
        mask = occupied[source * CORES + core] > 0
        new[source] = jnp.where(mask, MOMENTUM_RATE * kept + grad, kept)
    for k in range(chips):
        value = new[lax.rem(chip ^ k, sources)]
        if k == 0:
            here[...] = value
        else:
            encode(value, away[k - 1])


def refreshed_rows(index, occupied, old, near, arrived, chips):
    _, cols, width = old.shape
    coded = jax.ShapeDtypeStruct((cols + SCALE_ROWS, width), jnp.int16)
    return pl.pallas_call(
        functools.partial(refresh_kernel, chips),
        in_specs=[SMEM, SMEM] + [VMEM] * (2 + len(arrived)),
        out_specs=[VMEM] * (1 + chips),
        out_shape=[
            jax.ShapeDtypeStruct(old.shape, jnp.float32),
            jax.ShapeDtypeStruct((cols, width), jnp.float32),
        ]
        + [coded] * (chips - 1),
        compiler_params=PARAMS,
        name="refresh_momentum",
    )(index, occupied, old, near, *arrived)


def back_kernel(index, new, own, sibling, both):
    core = index[0]
    rows = own.shape[1]
    for s in range(own.shape[0]):
        both[...] = new[s].T
        own[s] = both[pl.ds(pl.multiple_of(core * rows, 16), rows)]
        sibling[s] = both[pl.ds(pl.multiple_of((1 - core) * rows, 16), rows)]


def turn_back(index, new):
    sources, cols, width = new.shape
    half = jax.ShapeDtypeStruct((sources, width // CORES, cols), jnp.float32)
    return pl.pallas_call(
        back_kernel,
        in_specs=[SMEM, VMEM],
        out_specs=[VMEM, VMEM],
        out_shape=[half, half],
        scratch_shapes=[pltpu.VMEM((width, cols), jnp.float32)],
        compiler_params=PARAMS,
        name="turn_back",
    )(index, new)


def merge_kernel(index, own, sibling, out):
    core = index[0]
    for s in range(own.shape[0]):
        out[s * CORES + core] = own[s]
        out[s * CORES + 1 - core] = sibling[s]


def merge(index, own, sibling):
    sources, rows, cols = own.shape
    return pl.pallas_call(
        merge_kernel,
        in_specs=[SMEM, VMEM, VMEM],
        out_specs=VMEM,
        out_shape=jax.ShapeDtypeStruct((sources * CORES, rows, cols), jnp.float32),
        compiler_params=PARAMS,
        name="merge_momentum",
    )(index, own, sibling)


def fold_rows(rows):
    return 2 if rows % 32 == 0 else 1


def newton_kernel(chips, index, here, *refs):
    away, outs, (matrix, turned) = refs[: chips - 1], refs[chips - 1 : -2], refs[-2:]
    cols, width = here.shape
    matrix[:, :width] = here[...]
    for k in range(1, chips):
        matrix[:, k * width : (k + 1) * width] = decode(away[k - 1])
    value = matrix[...]
    norm = jnp.sqrt(jnp.sum(value * value)) + 1e-07
    iterate = (value / norm).astype(jnp.bfloat16)
    for _ in range(ITERS):
        gram = lax.dot_general(
            iterate, iterate, (((1,), (1,)), ((), ())), preferred_element_type=jnp.float32
        )
        square = lax.dot_general(
            gram, gram, (((1,), (0,)), ((), ())), precision=lax.Precision.HIGHEST,
            preferred_element_type=jnp.float32,
        )
        polynomial = (QUINTIC_B * gram + QUINTIC_C * square).T.astype(jnp.bfloat16)
        product = lax.dot_general(
            polynomial, iterate, (((1,), (0,)), ((), ())), preferred_element_type=jnp.float32
        )
        iterate = (QUINTIC_A * iterate.astype(jnp.float32) + product).astype(jnp.bfloat16)
    matrix[...] = iterate.astype(jnp.float32)
    core = index[0]
    rows = width // CORES
    fold = fold_rows(rows)
    for k in range(chips):
        turned[...] = matrix[:, k * width : (k + 1) * width].T
        for c in range(CORES):
            out = outs[k * CORES + c]
            for f in range(fold):
                first = (core ^ c) * rows + f * (rows // fold)
                part = turned[pl.ds(pl.multiple_of(first, 8), rows // fold)]
                out[:, f * cols : (f + 1) * cols] = part.astype(jnp.bfloat16)


def newton(index, here, away):
    cols, width = here.shape
    chips = len(away) + 1
    rows = width // CORES
    fold = fold_rows(rows)
    block = jax.ShapeDtypeStruct((rows // fold, fold * cols), jnp.bfloat16)
    return pl.pallas_call(
        functools.partial(newton_kernel, chips),
        in_specs=[SMEM] + [VMEM] * chips,
        out_specs=[VMEM] * (chips * CORES),
        out_shape=[block] * (chips * CORES),
        scratch_shapes=[
            pltpu.VMEM((cols, chips * width), jnp.float32),
            pltpu.VMEM((width, cols), jnp.float32),
        ],
        compiler_params=PARAMS,
        name="newton_schulz",
    )(index, here, *away)


def weight_kernel(chips, sources, kn_count, index, occupied, gamma, root, weight, *refs):
    blocks, out = refs[:-1], refs[-1]
    _, rows, cols = weight.shape
    fold = blocks[0].shape[1] // cols
    step_size = 0.04 * math.sqrt(max(rows * chips * CORES, cols))
    core, chip = index[0], index[1]
    column = lax.broadcasted_iota(jnp.int32, (1, cols), 1)

    def update(k, c):
        slot = (chip ^ k) * CORES + (core ^ c)
        scale = jnp.where(column < kn_count, root[slot], gamma[slot])
        mask = occupied[slot] > 0
        part = rows // fold
        for f in range(fold):
            old = weight[slot, f * part : (f + 1) * part]
            value = blocks[k * CORES + c][:, f * cols : (f + 1) * cols].astype(jnp.float32)
            new = (WEIGHT_KEEP * old - step_size * value) * scale
            out[slot, f * part : (f + 1) * part] = jnp.where(mask, new, old)

    for k in range(chips):
        for c in range(CORES):
            if sources == chips:
                update(k, c)
            else:
                pl.when((chip ^ k) < sources)(functools.partial(update, k, c))


def weights(index, occupied, gamma, weight, blocks, kn_count):
    chips = len(blocks) // CORES
    sources = weight.shape[0] // CORES
    return pl.pallas_call(
        functools.partial(weight_kernel, chips, sources, kn_count),
        in_specs=[SMEM] * 4 + [VMEM] * (1 + len(blocks)),
        out_specs=VMEM,
        out_shape=jax.ShapeDtypeStruct(weight.shape, jnp.float32),
        compiler_params=PARAMS,
        name="update_weight",
    )(index, occupied, gamma, jnp.sqrt(gamma), weight, *blocks)


def body(grad_partials, assignment, momentum, q_weight, k_weight, max_logits):
    heads_own = grad_partials.shape[2]
    kn_count = k_weight.shape[2]
    sources = lax.axis_size("owner")
    devices = lax.axis_size("dp") * lax.axis_size("context")
    chips = devices // CORES
    owner = lax.axis_index("owner")
    device = lax.axis_index(PLANE)
    core, chip = device % CORES, device // CORES
    index = jnp.stack([core, chip, owner]).astype(jnp.int32)

    def swap(value, bits):
        return lax.ppermute(value, PLANE, [(i, i ^ bits) for i in range(devices)])

    target = assignment[:, 0]
    blocks = target.reshape(sources, heads_own)
    number = jnp.arange(heads_own, dtype=jnp.int32)
    earlier = (blocks[:, None, :] == blocks[:, :, None]) & (number[None, :] < number[:, None])[None]
    position = jnp.sum(earlier.astype(jnp.int32), axis=2)
    mine, my_position = (lax.dynamic_index_in_dim(a, owner, 0, False) for a in (blocks, position))
    to = owner ^ jnp.arange(sources, dtype=jnp.int32)
    places = jnp.arange(CORES, dtype=jnp.int32)
    chosen = (mine == to[None, :, None]) & (my_position == places[:, None, None])
    heads = jnp.sum(jnp.where(chosen, number, 0), axis=2)
    own_heads = lax.dynamic_index_in_dim(heads, core, 0, False)
    other_heads = lax.dynamic_index_in_dim(heads, 1 - core, 0, False)
    held = (blocks[:, None, :] == owner) & (position[:, None, :] == places[None, :, None])
    occupied = jnp.any(held, axis=2).reshape(-1)

    old = momentum.reshape((sources, CORES) + momentum.shape[1:])
    sibling_old = swap(lax.dynamic_index_in_dim(old, 1 - core, 1, False), 1)

    g = jnp.transpose(grad_partials[0], (1, 2, 0))
    width = g.shape[2] // chips
    if width % 128:
        g = jnp.transpose(g.reshape(g.shape[:2] + (chips, width)), (0, 2, 1, 3))
    order = list(range(sources))[::-1]
    size = sources // CHUNKS
    near, arrived = None, {}
    for at in range(0, sources, size):
        ks = order[at : at + size]
        outgoing = jnp.stack([lax.dynamic_index_in_dim(g, other_heads[k], 0, False) for k in ks])
        sibling = swap(outgoing, 1)
        here, *away = pair_sums(g, sibling, jnp.stack([own_heads[k] for k in ks]), chip, chips)
        away = [swap(value, CORES * (k + 1)) for k, value in enumerate(away)]
        totals = plane_sums(here, away, [k == 0 for k in ks])
        for k, total in zip(ks, totals):
            if k == 0:
                near = total
            else:
                arrived[k] = lax.ppermute(total, "owner", [(i, i ^ k) for i in range(sources)])

    peak = max_logits
    parts = lax.axis_size("context")
    bit = 1
    while bit < parts:
        peak = jnp.maximum(peak, lax.ppermute(peak, "context", [(i, i ^ bit) for i in range(parts)]))
        bit *= 2
    gamma = jnp.minimum(1.0, LOGIT_CAP / peak[0]).reshape(sources, heads_own)
    home_gamma = lax.dynamic_index_in_dim(gamma, owner, 0, False)
    slot_gamma = jnp.sum(jnp.where(held, gamma[:, None, :], 0.0), axis=2).reshape(-1)
    k_weight_out = k_weight * jnp.sqrt(home_gamma)[:, None, None]

    occupied = occupied.astype(jnp.int32)
    turned = turn(index, momentum, sibling_old)
    new, here, *away = refreshed_rows(
        index, occupied, turned, near, [arrived[k] for k in range(1, sources)], chips
    )
    away = [swap(value, CORES * (k + 1)) for k, value in enumerate(away)]
    own_new, sibling_new = turn_back(index, new)
    momentum_out = merge(index, own_new, swap(sibling_new, 1))

    results = newton(index, here, away)
    results = [value if bits == 0 else swap(value, bits) for bits, value in enumerate(results)]
    q_weight_out = weights(index, occupied, slot_gamma, q_weight, results, kn_count)
    return (momentum_out, q_weight_out, k_weight_out)


def solution(mesh):
    rows = P("owner", ("dp", "context"), None)
    return jax.shard_map(
        body,
        mesh=mesh,
        in_specs=(
            P(("dp", "context"), None, "owner", None),
            P(),
            rows,
            rows,
            rows,
            P("context", None),
        ),
        out_specs=(rows, rows, rows),
        check_vma=False,
    )
```

```python
import functools
import math

import jax
import jax.numpy as jnp
from jax import lax
from jax.experimental import pallas as pl
from jax.experimental.pallas import tpu as pltpu
from jax.sharding import PartitionSpec as P

ITERS = 2
MOMENTUM_RATE = 0.95
WEIGHT_KEEP = 0.98
LOGIT_CAP = 100.0
QUINTIC_A = 3.4445
QUINTIC_B = -4.775
QUINTIC_C = 2.0315

CORES = 2
PLANE = ("dp", "context")
SCALE_ROWS = 16
LEVELS = 14.99
STEPS = 8.0
LEFT = 128

SMEM = pl.BlockSpec(memory_space=pltpu.SMEM)
VMEM = pl.BlockSpec(memory_space=pltpu.VMEM)
ANY = pl.BlockSpec(memory_space=pl.ANY)
PARAMS = pltpu.CompilerParams(vmem_limit_bytes=48 * 1024 * 1024)


def whereabouts():
    device = lax.axis_index("dp") * lax.axis_size("context") + lax.axis_index("context")
    return lax.axis_index("owner"), device // CORES, device % CORES


def head_of(assignment, block, who, place, heads_own):
    found, seen = 0, 0
    for i in range(heads_own):
        hit = (assignment[0, block * heads_own + i] == who).astype(jnp.int32)
        found = jnp.where((hit == 1) & (seen == place), i, found)
        seen = seen + hit
    return found, seen


def encode(parts, out):
    top = functools.reduce(jnp.maximum, [jnp.max(jnp.abs(p), axis=0, keepdims=True) for p in parts])
    level = jnp.clip(jnp.ceil(STEPS * jnp.log2(top)), -100.0 * STEPS, 128.0 * STEPS)
    factor = jnp.exp2(LEVELS - level * (1.0 / STEPS))
    at = 0
    for p in parts:
        out[at : at + p.shape[0]] = jnp.round(p * factor).astype(jnp.int32).astype(jnp.int16)
        at += p.shape[0]
    rows = jnp.broadcast_to(level, (SCALE_ROWS, level.shape[1]))
    out[at:] = rows.astype(jnp.int32).astype(jnp.int16)


def decode(block, count):
    size = (block.shape[0] - SCALE_ROWS) // count
    level = block[size * count :].astype(jnp.int32).astype(jnp.float32)[0:1]
    factor = jnp.exp2(level * (1.0 / STEPS) - LEVELS)
    return [
        block[i * size : (i + 1) * size].astype(jnp.int32).astype(jnp.float32) * factor
        for i in range(count)
    ]


def fetch_kernel(heads_own, wanted, with_momentum, assignment, g, momentum, *refs):
    owner, _, core = whereabouts()
    outs, sem = refs[:-1], refs[-1]
    copies = []
    for group, out in zip(wanted, outs):
        for i, (k, other) in enumerate(group):
            place = 1 - core if other else core
            head, _ = head_of(assignment, owner, owner ^ k, place, heads_own)
            copies.append((g.at[head], out.at[i]))
    if with_momentum:
        for s in range(outs[-1].shape[0]):
            copies.append((momentum.at[s * CORES + 1 - core], outs[-1].at[s]))
    copies = [pltpu.make_async_copy(a, b, sem.at[i]) for i, (a, b) in enumerate(copies)]
    for copy in copies:
        copy.start()
    for copy in copies:
        copy.wait()


def fetch(assignment, g, momentum, wanted, with_momentum):
    out_shape = [jax.ShapeDtypeStruct((len(group),) + g.shape[1:], g.dtype) for group in wanted]
    count = sum(len(group) for group in wanted)
    if with_momentum:
        sources = momentum.shape[0] // CORES
        out_shape.append(jax.ShapeDtypeStruct((sources,) + momentum.shape[1:], momentum.dtype))
        count += sources
    return pl.pallas_call(
        functools.partial(fetch_kernel, g.shape[0], wanted, with_momentum),
        in_specs=[SMEM, ANY, ANY],
        out_specs=[VMEM] * len(out_shape),
        out_shape=out_shape,
        scratch_shapes=[pltpu.SemaphoreType.DMA((count,))],
        compiler_params=PARAMS,
        name="fetch_heads",
    )(assignment, g, momentum)


def offsets(bits):
    result = [0]
    for bit in reversed(bits):
        result = result + [r | (1 << bit) for r in result]
    return result


def pair_kernel(orders, aligned, own, sibling, *outs):
    _, chip, _ = whereabouts()
    width = outs[0].shape[-1]
    for a, bits in enumerate(orders):
        keep, away = outs[2 * a : 2 * a + 2]
        blocks = []
        for offset in offsets(bits):
            to = chip ^ offset
            if aligned:
                rows = pl.ds(pl.multiple_of(to * width, 128), width)
                first, second = own[a, :, rows], sibling[a, :, rows]
            else:
                first, second = own[a, to], sibling[a, to]
            blocks.append(first.astype(jnp.float32) + second.astype(jnp.float32))
            if len(blocks) <= keep.shape[0]:
                keep[len(blocks) - 1] = blocks[-1]
        encode(blocks[keep.shape[0] :], away)


def halves(count, cols, width):
    return [
        jax.ShapeDtypeStruct((count, cols, width), jnp.float32),
        jax.ShapeDtypeStruct((count * cols + SCALE_ROWS, width), jnp.int16),
    ]


def pair_sums(own, sibling, orders, chips):
    aligned = own.ndim == 3
    cols = own.shape[-2]
    width = own.shape[-1] // chips if aligned else own.shape[-1]
    return pl.pallas_call(
        functools.partial(pair_kernel, orders, aligned),
        in_specs=[VMEM, VMEM],
        out_specs=[VMEM] * 4,
        out_shape=halves(chips // 2, cols, width) * 2,
        compiler_params=PARAMS,
        name="pair_sum",
    )(own, sibling)


def plane_kernel(plain, *refs):
    outs = list(refs[4:])
    for a in range(2):
        keep, away = refs[2 * a : 2 * a + 2]
        count = keep.shape[0]
        blocks = [keep[i] + part for i, part in enumerate(decode(away, count))]
        if count > 1:
            half = outs.pop(0)
            for i in range(count // 2):
                half[i] = blocks[i]
            encode(blocks[count // 2 :], outs.pop(0))
        elif plain[a]:
            outs.pop(0)[...] = blocks[0]
        else:
            encode(blocks, outs.pop(0))


def plane_sums(state, plain):
    count, cols, width = state[0].shape
    if count > 1:
        out_shape = halves(count // 2, cols, width) * 2
    else:
        coded = jax.ShapeDtypeStruct((cols + SCALE_ROWS, width), jnp.int16)
        out_shape = [jax.ShapeDtypeStruct((cols, width), jnp.float32) if p else coded for p in plain]
    return pl.pallas_call(
        functools.partial(plane_kernel, plain),
        in_specs=[VMEM] * 4,
        out_specs=[VMEM] * len(out_shape),
        out_shape=out_shape,
        compiler_params=PARAMS,
        name="plane_sum",
    )(*state)


def turn_kernel(own, sibling, out, both):
    _, _, core = whereabouts()
    rows = own.shape[1]
    for s in range(sibling.shape[0]):
        both[pl.ds(pl.multiple_of(core * rows, 16), rows)] = own[s * CORES + core]
        both[pl.ds(pl.multiple_of((1 - core) * rows, 16), rows)] = sibling[s]
        out[s] = both[...].T


def turn(own, sibling):
    sources, rows, cols = sibling.shape
    return pl.pallas_call(
        turn_kernel,
        in_specs=[VMEM, VMEM],
        out_specs=VMEM,
        out_shape=jax.ShapeDtypeStruct((sources, cols, CORES * rows), jnp.float32),
        scratch_shapes=[pltpu.VMEM((CORES * rows, cols), jnp.float32)],
        compiler_params=PARAMS,
        name="turn_momentum",
    )(own, sibling)


def pack(matrix, out):
    cols = matrix.shape[0]
    rest = cols - LEFT
    out[:cols] = matrix[:, :LEFT].astype(out.dtype)
    for f in range(2):
        part = matrix[LEFT + f * rest // 2 : LEFT + (f + 1) * rest // 2, LEFT:]
        out[cols : cols + rest // 2, f * rest : (f + 1) * rest] = part.astype(out.dtype)


def unpack(packed, out):
    cols = out.shape[0]
    rest = cols - LEFT
    out[:, :LEFT] = packed[:cols]
    out[:LEFT, LEFT:] = packed[LEFT:cols].T
    for f in range(2):
        part = packed[cols : cols + rest // 2, f * rest : (f + 1) * rest]
        out[LEFT + f * rest // 2 : LEFT + (f + 1) * rest // 2, LEFT:] = part


def gram_kernel(chips, heads_own, assignment, old, near, *refs):
    sources = old.shape[0]
    arrived, refs = refs[: sources - 1], refs[sources - 1 :]
    (new, here), away, packed = refs[:2], refs[2:-1], refs[-1]
    owner, chip, core = whereabouts()
    for k in range(sources):
        source = owner ^ k
        grad = near[...] if k == 0 else decode(arrived[k - 1], 1)[0]
        kept = old[source]
        _, held = head_of(assignment, source, owner, 0, heads_own)
        new[source] = jnp.where(held > core, MOMENTUM_RATE * kept + grad, kept)
    for k in range(chips):
        value = new[lax.rem(chip ^ k, sources)].astype(jnp.bfloat16)
        gram = lax.dot_general(
            value, value, (((1,), (1,)), ((), ())), preferred_element_type=jnp.float32
        )
        if k == 0:
            pack(gram, here)
        else:
            pack(gram, packed)
            encode([packed[...]], away[k - 1])


def grams(assignment, old, near, arrived, chips, heads_own):
    cols = old.shape[1]
    rows = cols + (cols - LEFT) // 2
    coded = jax.ShapeDtypeStruct((rows + SCALE_ROWS, LEFT), jnp.int16)
    return pl.pallas_call(
        functools.partial(gram_kernel, chips, heads_own),
        in_specs=[SMEM] + [VMEM] * (2 + len(arrived)),
        out_specs=[VMEM] * (1 + chips),
        out_shape=[
            jax.ShapeDtypeStruct(old.shape, jnp.float32),
            jax.ShapeDtypeStruct((rows, LEFT), jnp.float32),
        ]
        + [coded] * (chips - 1),
        scratch_shapes=[pltpu.VMEM((rows, LEFT), jnp.float32)],
        compiler_params=PARAMS,
        name="refresh_and_gram",
    )(assignment, old, near, *arrived)


def small_dot(a, b):
    return lax.dot_general(
        a.astype(jnp.bfloat16), b.astype(jnp.bfloat16), (((1,), (0,)), ((), ())),
        preferred_element_type=jnp.float32,
    )


def newton_kernel(here, *refs):
    away, (out, square) = refs[:-2], refs[-2:]
    cols = square.shape[0]
    total = here[...]
    for block in away:
        total = total + decode(block, 1)[0]
    unpack(total, square)
    gram = square[...]
    row = lax.broadcasted_iota(jnp.int32, gram.shape, 0)
    column = lax.broadcasted_iota(jnp.int32, gram.shape, 1)
    square_sum = jnp.sum(jnp.where(row == column, gram, 0.0), axis=(0, 1), keepdims=True)
    norm = jnp.sqrt(square_sum) + 1e-07
    inverse = 1.0 / norm
    gram = jnp.where(norm < jnp.inf, gram * inverse * inverse, 0.0)
    first = QUINTIC_B * gram + QUINTIC_C * small_dot(gram, gram)
    twice = (2.0 * QUINTIC_A) * first + small_dot(first, first)
    gram = (QUINTIC_A * QUINTIC_A) * gram + small_dot(gram, twice)
    second = QUINTIC_B * gram + QUINTIC_C * small_dot(gram, gram)
    result = QUINTIC_A * (first + second) + small_dot(first, second)
    pack(result, out)
    high = norm.astype(jnp.bfloat16).astype(jnp.float32)
    middle = (norm - high).astype(jnp.bfloat16).astype(jnp.float32)
    low = norm - high - middle
    row = lax.broadcasted_iota(jnp.int32, (SCALE_ROWS, LEFT), 0)
    scales = jnp.where(row == 0, high, jnp.where(row == 1, middle, jnp.where(row == 2, low, 0.0)))
    out[out.shape[0] - SCALE_ROWS :] = scales.astype(jnp.bfloat16)


def newton(here, away, cols):
    return pl.pallas_call(
        newton_kernel,
        in_specs=[VMEM] * (1 + len(away)),
        out_specs=VMEM,
        out_shape=jax.ShapeDtypeStruct((here.shape[0] + SCALE_ROWS, LEFT), jnp.bfloat16),
        scratch_shapes=[pltpu.VMEM((cols, cols), jnp.float32)],
        compiler_params=PARAMS,
        name="newton_schulz",
    )(here, *away)


def back_kernel(new, own, sibling, both):
    _, _, core = whereabouts()
    rows = own.shape[1]
    for s in range(own.shape[0]):
        both[...] = new[s].T
        own[s] = both[pl.ds(pl.multiple_of(core * rows, 16), rows)]
        sibling[s] = both[pl.ds(pl.multiple_of((1 - core) * rows, 16), rows)]


def turn_back(new):
    sources, cols, width = new.shape
    half = jax.ShapeDtypeStruct((sources, width // CORES, cols), jnp.float32)
    return pl.pallas_call(
        back_kernel,
        in_specs=[VMEM],
        out_specs=[VMEM, VMEM],
        out_shape=[half, half],
        scratch_shapes=[pltpu.VMEM((width, cols), jnp.float32)],
        compiler_params=PARAMS,
        name="turn_back",
    )(new)


def merge_kernel(own, sibling, out):
    _, _, core = whereabouts()
    for s in range(own.shape[0]):
        out[s * CORES + core] = own[s]
        out[s * CORES + 1 - core] = sibling[s]


def merge(own, sibling):
    sources, rows, cols = own.shape
    return pl.pallas_call(
        merge_kernel,
        in_specs=[VMEM, VMEM],
        out_specs=VMEM,
        out_shape=jax.ShapeDtypeStruct((sources * CORES, rows, cols), jnp.float32),
        compiler_params=PARAMS,
        name="merge_momentum",
    )(own, sibling)


def head_scale(peak, head, shape):
    return jnp.minimum(1.0, LOGIT_CAP / jnp.full(shape, peak[0, head], jnp.float32))


def weight_kernel(chips, heads_own, kn_count, rows_all, assignment, peak, momentum, weight, *refs):
    blocks, (out, matrix) = refs[:-2], refs[-2:]
    slots, _, cols = weight.shape
    sources = slots // CORES
    step_size = 0.04 * math.sqrt(max(rows_all, cols))
    owner, chip, core = whereabouts()
    column = lax.broadcasted_iota(jnp.int32, (1, cols), 1)

    def update(k, c):
        source, place = chip ^ k, core ^ c
        slot = source * CORES + place
        head, held = head_of(assignment, source, owner, place, heads_own)
        block = blocks[c * chips + k]
        parts = block[block.shape[0] - SCALE_ROWS :].astype(jnp.float32)
        norm = parts[0:1, 0:1] + parts[1:2, 0:1] + parts[2:3, 0:1]
        unpack(block[: block.shape[0] - SCALE_ROWS].astype(jnp.float32), matrix)
        start = (momentum[slot] / norm).astype(jnp.bfloat16)
        result = (QUINTIC_A * QUINTIC_A) * start.astype(jnp.float32) + small_dot(start, matrix[...])
        gamma = head_scale(peak, source * heads_own + head, (1, cols))
        scale = jnp.where(column < kn_count, jnp.sqrt(gamma), gamma)
        old = weight[slot]
        new = (WEIGHT_KEEP * old - step_size * result) * scale
        out[slot] = jnp.where(held > place, new, old)

    for c in range(CORES):
        for k in range(chips):
            if sources == chips:
                update(k, c)
            else:
                pl.when((chip ^ k) < sources)(functools.partial(update, k, c))


def weights(assignment, peak, momentum, weight, blocks, heads_own, kn_count):
    chips = len(blocks) // CORES
    _, rows, cols = weight.shape
    return pl.pallas_call(
        functools.partial(weight_kernel, chips, heads_own, kn_count, rows * chips * CORES),
        in_specs=[SMEM] * 2 + [VMEM] * (2 + len(blocks)),
        out_specs=VMEM,
        out_shape=jax.ShapeDtypeStruct(weight.shape, jnp.float32),
        scratch_shapes=[pltpu.VMEM((cols, cols), jnp.float32)],
        compiler_params=PARAMS,
        name="update_weight",
    )(assignment, peak, momentum, weight, *blocks)


def key_kernel(peak, weight, out):
    owner, _, _ = whereabouts()
    heads_own, _, cols = weight.shape
    for i in range(heads_own):
        gamma = head_scale(peak, owner * heads_own + i, (1, cols))
        out[i] = weight[i] * jnp.sqrt(gamma)


def keys(peak, weight):
    return pl.pallas_call(
        key_kernel,
        in_specs=[SMEM, VMEM],
        out_specs=VMEM,
        out_shape=jax.ShapeDtypeStruct(weight.shape, jnp.float32),
        compiler_params=PARAMS,
        name="scale_keys",
    )(peak, weight)


def body(grad_partials, assignment, momentum, q_weight, k_weight, max_logits):
    heads_own = grad_partials.shape[2]
    sources = lax.axis_size("owner")
    devices = lax.axis_size("dp") * lax.axis_size("context")
    chips = devices // CORES
    levels = chips.bit_length() - 1
    orders = (list(range(levels)), list(range(levels))[::-1])
    assignment = assignment.T

    def swap(value, bits):
        return lax.ppermute(value, PLANE, [(i, i ^ bits) for i in range(devices)])

    g = jnp.transpose(grad_partials[0], (1, 2, 0))
    if (g.shape[2] // chips) % 128:
        g = jnp.transpose(g.reshape(g.shape[:2] + (chips, g.shape[2] // chips)), (0, 2, 1, 3))
    order = list(range(sources))[::-1]
    pairs = [order[at : at + 2] for at in range(0, sources, 2)]
    others = {}
    (others[0],) = fetch(assignment, g, momentum, [[(k, True) for k in pairs[0]]], False)
    wanted = [[(k, True) for k in pair] for pair in pairs[1:]]
    wanted += [[(k, False) for k in pair] for pair in pairs]
    *fetched, outgoing = fetch(assignment, g, momentum, wanted, True)
    for i in range(1, len(pairs)):
        others[i] = fetched[i - 1]
    own = fetched[len(pairs) - 1 :]

    near, arrived = None, {}
    peak = max_logits
    sibling_old = None
    for i, ks in enumerate(pairs):
        sibling = swap(others[i], 1)
        if i == 1:
            parts = lax.axis_size("context")
            bit = 1
            while bit < parts:
                perm = [(j, j ^ bit) for j in range(parts)]
                peak = jnp.maximum(peak, lax.ppermute(peak, "context", perm))
                bit *= 2
            sibling_old = swap(outgoing, 1)
            sibling, peak = lax.optimization_barrier((sibling, peak))
        state = list(pair_sums(own[i], sibling, orders, chips))
        for level in range(levels):
            for a in range(2):
                state[2 * a + 1] = swap(state[2 * a + 1], CORES << orders[a][level])
            state = list(plane_sums(state, [k == 0 for k in ks]))
        for k, total in zip(ks, state):
            if k == 0:
                near = total
            else:
                arrived[k] = lax.ppermute(total, "owner", [(j, j ^ k) for j in range(sources)])

    turned = turn(momentum, sibling_old)
    arrived = [arrived[k] for k in range(1, sources)]
    new, here, *away = grams(assignment, turned, near, arrived, chips, heads_own)
    away = [swap(value, CORES * (k + 1)) for k, value in enumerate(away)]
    own_new, sibling_new = turn_back(new)
    momentum_out = merge(own_new, swap(sibling_new, 1))
    k_weight_out = keys(peak, k_weight)

    result = newton(here, away, momentum.shape[2])
    results = [result] + [swap(result, CORES * k) for k in range(1, chips)]
    results += [swap(value, 1) for value in results]
    q_weight_out = weights(
        assignment, peak, momentum_out, q_weight, results, heads_own, k_weight.shape[2]
    )
    return (momentum_out, q_weight_out, k_weight_out)


def solution(mesh):
    rows = P("owner", ("dp", "context"), None)
    return jax.shard_map(
        body,
        mesh=mesh,
        in_specs=(
            P(("dp", "context"), None, "owner", None),
            P(),
            rows,
            rows,
            rows,
            P("context", None),
        ),
        out_specs=(rows, rows, rows),
        check_vma=False,
    )
```

```python
import functools
import math

import jax
import jax.numpy as jnp
from jax import lax
from jax.experimental import pallas as pl
from jax.experimental.pallas import tpu as pltpu
from jax.sharding import PartitionSpec as P

ITERS = 2
MOMENTUM_RATE = 0.95
WEIGHT_KEEP = 0.98
LOGIT_CAP = 100.0
QUINTIC_A = 3.4445
QUINTIC_B = -4.775
QUINTIC_C = 2.0315

CORES = 2
PLANE = ("dp", "context")
SCALE_ROWS = 16
LEVELS = 14.99
STEPS = 8.0
NOTE_UNITS = (64.0, 64.0 * 32768.0, 64.0 * 32768.0 * 32768.0)
GROUPS = 4
LEFT = 128

SMEM = pl.BlockSpec(memory_space=pltpu.SMEM)
VMEM = pl.BlockSpec(memory_space=pltpu.VMEM)
ANY = pl.BlockSpec(memory_space=pl.ANY)
HBM = pl.BlockSpec(memory_space=pltpu.HBM)
PARAMS = pltpu.CompilerParams(vmem_limit_bytes=36 * 1024 * 1024)
FIRST = pltpu.CompilerParams(vmem_limit_bytes=52 * 1024 * 1024)
SECOND = pltpu.CompilerParams(vmem_limit_bytes=44 * 1024 * 1024)


def whereabouts():
    device = lax.axis_index("dp") * lax.axis_size("context") + lax.axis_index("context")
    return lax.axis_index("owner"), device // CORES, device % CORES


def call(kernel, name, ins, outs, scratch=(), after=(), aliases=None, params=PARAMS):
    count = len(ins)

    def whole(*refs):
        kernel(*refs[:count], *refs[count + len(after) :])

    return pl.pallas_call(
        whole,
        in_specs=[spec for spec, _ in ins] + [ANY] * len(after),
        out_specs=[spec for spec, _, _ in outs],
        out_shape=[jax.ShapeDtypeStruct(shape, dtype) for _, shape, dtype in outs],
        scratch_shapes=list(scratch),
        input_output_aliases=aliases or {},
        compiler_params=params,
        name=name,
    )(*[array for _, array in ins], *after)


def head_of(assignment, block, who, place, heads_own):
    found, seen = 0, 0
    for i in range(heads_own):
        hit = (assignment[0, block * heads_own + i] == who).astype(jnp.int32)
        found = jnp.where((hit == 1) & (seen == place), i, found)
        seen = seen + hit
    return found, seen


def encode(parts, out, note=None):
    top = functools.reduce(jnp.maximum, [jnp.max(jnp.abs(p), axis=0, keepdims=True) for p in parts])
    level = jnp.clip(jnp.ceil(STEPS * jnp.log2(top)), -100.0 * STEPS, 128.0 * STEPS)
    factor = jnp.exp2(LEVELS - level * (1.0 / STEPS))
    at = 0
    for p in parts:
        out[at : at + p.shape[0]] = jnp.round(p * factor).astype(jnp.int32).astype(jnp.int16)
        at += p.shape[0]
    rows = jnp.broadcast_to(level, (SCALE_ROWS, level.shape[1]))
    if note is not None:
        row = lax.broadcasted_iota(jnp.int32, rows.shape, 0)
        rest = note * NOTE_UNITS[0]
        for i, unit in enumerate(NOTE_UNITS):
            whole = jnp.floor(rest)
            rows = jnp.where(row == i + 1, whole, rows)
            rest = (rest - whole) * 32768.0
    out[at:] = rows.astype(jnp.int32).astype(jnp.int16)


def noted(block, width):
    rows = block[block.shape[0] - SCALE_ROWS :].astype(jnp.int32).astype(jnp.float32)
    parts = [rows[i + 1 : i + 2, :width] / unit for i, unit in enumerate(NOTE_UNITS)]
    return parts[0] + (parts[1] + parts[2])


def decode(block, count):
    size = (block.shape[0] - SCALE_ROWS) // count
    level = block[size * count :].astype(jnp.int32).astype(jnp.float32)[0:1]
    factor = jnp.exp2(level * (1.0 / STEPS) - LEVELS)
    return [
        block[i * size : (i + 1) * size].astype(jnp.int32).astype(jnp.float32) * factor
        for i in range(count)
    ]


def fetch_kernel(heads_own, wanted, assignment, g, *refs):
    owner, _, core = whereabouts()
    token, outs, sem = refs[-2], refs[:-2], refs[-1]
    token[...] = jnp.zeros_like(token)
    copies = []
    for group, out in zip(wanted, outs[-len(wanted) :]):
        for i, (k, other) in enumerate(group):
            place = 1 - core if other else core
            head, _ = head_of(assignment, owner, owner ^ k, place, heads_own)
            copies.append(pltpu.make_async_copy(g.at[head], out.at[i], sem.at[len(copies)]))
            copies[-1].start()
    if len(outs) > len(wanted):
        momentum, logits, old = outs[:3]
        cols = momentum.shape[2]
        for s in range(old.shape[0]):
            old[s, :, :cols] = momentum[s * CORES + 1 - core]
        old[0, 0:1, cols : cols + logits.shape[1]] = logits[...]
    for copy in copies:
        copy.wait()


def fetch(assignment, g, wanted, rest=(), after=()):
    outs = [(VMEM, (len(group),) + g.shape[1:], g.dtype) for group in wanted]
    count = sum(len(group) for group in wanted)
    ins = [(SMEM, assignment), (ANY, g)]
    outs.append((VMEM, (8, LEFT), jnp.float32))
    if rest:
        momentum, logits = rest
        slots, rows, _ = momentum.shape
        outs = [(VMEM, (slots // CORES, rows, 2 * LEFT), momentum.dtype)] + outs
        ins += [(VMEM, momentum), (VMEM, logits)]
    return call(
        functools.partial(fetch_kernel, g.shape[0], wanted),
        "fetch_heads",
        ins,
        outs,
        [pltpu.SemaphoreType.DMA((count,))],
        after,
        params=SECOND if after else FIRST,
    )


def pair_kernel(chips, aligned, heads, passed, own, sibling, *refs):
    _, chip, _ = whereabouts()
    note = None
    refs = refs[passed : len(refs) - passed] if passed else refs
    if len(refs) > chips:
        logits, padded = refs[0], refs[-1]
        padded[...] = jnp.zeros_like(padded)
        padded[:, : logits.shape[1]] = logits[...]
        note, refs = padded[...], refs[1:-1]
    here, away = refs[0], refs[1:]
    width = here.shape[-1]
    for k in range(chips):
        to = chip ^ k
        blocks = []
        for mine, theirs in heads:
            if aligned:
                rows = pl.ds(pl.multiple_of(to * width, 128), width)
                first, second = own[mine, :, rows], sibling[theirs, :, rows]
            else:
                first, second = own[mine, to], sibling[theirs, to]
            blocks.append(first.astype(jnp.float32) + second.astype(jnp.float32))
        if k == 0:
            for i, block in enumerate(blocks):
                here[i] = block
        else:
            encode(blocks, away[k - 1], note if k == 1 else None)


def pair_sums(own, sibling, heads, chips, after, note, passed):
    aligned = own.ndim == 3
    cols = own.shape[-2]
    width = own.shape[-1] // chips if aligned else own.shape[-1]
    coded = (VMEM, (len(heads) * cols + SCALE_ROWS, width), jnp.int16)
    outs = [(VMEM, (len(heads), cols, width), jnp.float32)] + [coded] * (chips - 1)
    return call(
        functools.partial(pair_kernel, chips, aligned, heads, len(passed)),
        "pair_sum",
        [(VMEM, own), (VMEM, sibling)]
        + [(ANY, value) for value in passed]
        + [(VMEM, value) for value in note],
        outs + [(ANY, value.shape, value.dtype) for value in passed],
        [pltpu.VMEM((1, width), jnp.float32) for _ in note],
        after=after,
        aliases={2 + i: chips + i for i in range(len(passed))},
    )


def plane_kernel(plain, noting, here, *refs):
    outs = refs[-len(plain) - noting :]
    away = refs[: len(refs) - len(outs)]
    if noting:
        logits, away = away[-1], away[:-1]
        peak, outs = outs[-1], outs[:-1]
        peak[...] = jnp.maximum(logits[...], noted(away[0], logits.shape[1]))
    blocks = [here[i] for i in range(len(plain))]
    for value in away:
        blocks = [a + b for a, b in zip(blocks, decode(value, len(plain)))]
    for is_plain, block, out in zip(plain, blocks, outs):
        if is_plain:
            out[...] = block
        else:
            encode([block], out)


def plane_sums(here, away, plain, after, note):
    _, cols, width = here.shape
    coded = (VMEM, (cols + SCALE_ROWS, width), jnp.int16)
    outs = [(VMEM, (cols, width), jnp.float32) if p else coded for p in plain]
    return call(
        functools.partial(plane_kernel, plain, len(note)),
        "plane_sum",
        [(VMEM, value) for value in (here, *away, *note)],
        outs + [(VMEM, value.shape, value.dtype) for value in note],
        after=after,
    )


def turn_kernel(own, sibling, logits, out, peak, both):
    _, _, core = whereabouts()
    rows = own.shape[1]
    for s in range(sibling.shape[0]):
        both[pl.ds(pl.multiple_of(core * rows, 16), rows)] = own[s * CORES + core]
        both[pl.ds(pl.multiple_of((1 - core) * rows, 16), rows)] = sibling[s, :, : own.shape[2]]
        out[s] = both[...].T
    cols = own.shape[2]
    peak[...] = jnp.maximum(logits[...], sibling[0, 0:1, cols : cols + logits.shape[1]])


def turn(own, sibling, logits):
    sources = sibling.shape[0]
    _, rows, cols = own.shape
    return call(
        turn_kernel,
        "turn_momentum",
        [(VMEM, own), (VMEM, sibling), (VMEM, logits)],
        [(VMEM, (sources, cols, CORES * rows), jnp.float32), (VMEM, logits.shape, logits.dtype)],
        [pltpu.VMEM((CORES * rows, cols), jnp.float32)],
    )


def pack(matrix, out):
    cols = matrix.shape[0]
    rest = cols - LEFT
    out[:cols] = matrix[:, :LEFT].astype(out.dtype)
    for f in range(2):
        part = matrix[LEFT + f * rest // 2 : LEFT + (f + 1) * rest // 2, LEFT:]
        out[cols : cols + rest // 2, f * rest : (f + 1) * rest] = part.astype(out.dtype)


def unpack(packed, out):
    cols = out.shape[0]
    rest = cols - LEFT
    out[:, :LEFT] = packed[:cols]
    out[:LEFT, LEFT:] = packed[LEFT:cols].astype(jnp.float32).T.astype(out.dtype)
    for f in range(2):
        part = packed[cols : cols + rest // 2, f * rest : (f + 1) * rest]
        out[LEFT + f * rest // 2 : LEFT + (f + 1) * rest // 2, LEFT:] = part


def gram_kernel(chips, heads_own, assignment, old, near, *refs):
    sources = old.shape[0]
    arrived, refs = refs[: sources - 1], refs[sources - 1 :]
    (new, here), away, packed = refs[:2], refs[2:-1], refs[-1]
    owner, chip, core = whereabouts()
    for k in range(sources):
        source = owner ^ k
        grad = near[...] if k == 0 else decode(arrived[k - 1], 1)[0]
        kept = old[source]
        _, held = head_of(assignment, source, owner, 0, heads_own)
        new[source] = jnp.where(held > core, MOMENTUM_RATE * kept + grad, kept)
    for k in range(chips):
        value = new[lax.rem(chip ^ k, sources)].astype(jnp.bfloat16)
        gram = lax.dot_general(
            value, value, (((1,), (1,)), ((), ())), preferred_element_type=jnp.float32
        )
        if k == 0:
            pack(gram, here)
        else:
            pack(gram, packed)
            encode([packed[...]], away[k - 1])


def grams(assignment, old, near, arrived, chips, heads_own, after):
    cols = old.shape[1]
    rows = cols + (cols - LEFT) // 2
    coded = (VMEM, (rows + SCALE_ROWS, LEFT), jnp.int16)
    return call(
        functools.partial(gram_kernel, chips, heads_own),
        "refresh_and_gram",
        [(SMEM, assignment)] + [(VMEM, value) for value in (old, near, *arrived)],
        [(VMEM, old.shape, jnp.float32), (VMEM, (rows, LEFT), jnp.float32)] + [coded] * (chips - 1),
        [pltpu.VMEM((rows, LEFT), jnp.float32)],
        after,
    )


def small_dot(a, b):
    return lax.dot_general(
        a.astype(jnp.bfloat16), b.astype(jnp.bfloat16), (((1,), (0,)), ((), ())),
        preferred_element_type=jnp.float32,
    )


def newton_kernel(here, *refs):
    away, (out, square) = refs[:-2], refs[-2:]
    cols = square.shape[0]
    total = here[...]
    for block in away:
        total = total + decode(block, 1)[0]
    unpack(total, square)
    gram = square[...]
    row = lax.broadcasted_iota(jnp.int32, gram.shape, 0)
    column = lax.broadcasted_iota(jnp.int32, gram.shape, 1)
    square_sum = jnp.sum(jnp.where(row == column, gram, 0.0), axis=(0, 1), keepdims=True)
    norm = jnp.sqrt(square_sum) + 1e-07
    inverse = 1.0 / norm
    gram = jnp.where(norm < jnp.inf, gram * inverse * inverse, 0.0)
    first = QUINTIC_B * gram + QUINTIC_C * small_dot(gram, gram)
    twice = (2.0 * QUINTIC_A) * first + small_dot(first, first)
    gram = (QUINTIC_A * QUINTIC_A) * gram + small_dot(gram, twice)
    second = QUINTIC_B * gram + QUINTIC_C * small_dot(gram, gram)
    result = QUINTIC_A * (first + second) + small_dot(first, second)
    pack(result, out)
    high = norm.astype(jnp.bfloat16).astype(jnp.float32)
    middle = (norm - high).astype(jnp.bfloat16).astype(jnp.float32)
    low = norm - high - middle
    row = lax.broadcasted_iota(jnp.int32, (SCALE_ROWS, LEFT), 0)
    scales = jnp.where(row == 0, high, jnp.where(row == 1, middle, jnp.where(row == 2, low, 0.0)))
    out[out.shape[0] - SCALE_ROWS :] = scales.astype(jnp.bfloat16)


def newton(here, away, cols, after):
    (out,) = call(
        newton_kernel,
        "newton_schulz",
        [(VMEM, value) for value in (here, *away)],
        [(VMEM, (here.shape[0] + SCALE_ROWS, LEFT), jnp.bfloat16)],
        [pltpu.VMEM((cols, cols), jnp.float32)],
        after,
    )
    return out


def back_kernel(new, own, sibling, both):
    _, _, core = whereabouts()
    rows = own.shape[1]
    for s in range(own.shape[0]):
        both[...] = new[s].T
        own[s] = both[pl.ds(pl.multiple_of(core * rows, 16), rows)]
        sibling[s] = both[pl.ds(pl.multiple_of((1 - core) * rows, 16), rows)]


def turn_back(new, after):
    sources, cols, width = new.shape
    half = (VMEM, (sources, width // CORES, cols), jnp.float32)
    return call(
        back_kernel,
        "turn_back",
        [(VMEM, new)],
        [half, half],
        [pltpu.VMEM((width, cols), jnp.float32)],
        after,
    )


def head_scale(peak, head, shape):
    return jnp.minimum(1.0, LOGIT_CAP / jnp.full(shape, peak[0, head], jnp.float32))


def base_kernel(heads_own, kn_count, assignment, peak, weight, out, scales):
    owner, _, _ = whereabouts()
    slots, _, cols = weight.shape
    column = lax.broadcasted_iota(jnp.int32, (1, cols), 1)
    for slot in range(slots):
        source, place = slot // CORES, slot % CORES
        head, held = head_of(assignment, source, owner, place, heads_own)
        gamma = head_scale(peak, source * heads_own + head, (1, cols))
        scale = jnp.where(column < kn_count, jnp.sqrt(gamma), gamma)
        old = weight[slot]
        out[slot] = jnp.where(held > place, (WEIGHT_KEEP * old) * scale, old)
        scales[slot : slot + 1] = jnp.where(held > place, scale, 0.0)


def bases(assignment, peak, weight, heads_own, kn_count):
    slots, _, cols = weight.shape
    return call(
        functools.partial(base_kernel, heads_own, kn_count),
        "scale_weight",
        [(SMEM, assignment), (SMEM, peak), (VMEM, weight)],
        [(VMEM, weight.shape, jnp.float32), (VMEM, (slots, cols), jnp.float32)],
    )


def weight_kernel(chips, other, rows_all, base, scales, momentum, *refs):
    blocks, refs = refs[:chips], refs[chips:]
    out, matrix, result, sem = refs[-4:]
    slots, _, cols = base.shape
    sources = slots // CORES
    step_size = 0.04 * math.sqrt(max(rows_all, cols))
    _, chip, core = whereabouts()
    place = 1 - core if other else core
    def written(k):
        return pltpu.make_async_copy(result.at[k], out.at[(chip ^ k) * CORES + place], sem.at[k])

    def update(k):
        source = chip ^ k
        slot = source * CORES + place
        block = blocks[k]
        parts = block[block.shape[0] - SCALE_ROWS :].astype(jnp.float32)
        norm = parts[0:1, 0:1] + parts[1:2, 0:1] + parts[2:3, 0:1]
        unpack(block[: block.shape[0] - SCALE_ROWS], matrix.at[k])
        start = (momentum[source] * (1.0 / norm)).astype(jnp.bfloat16)
        step = (QUINTIC_A * QUINTIC_A) * start.astype(jnp.float32) + small_dot(start, matrix[k])
        result[k] = base[slot] - step * (step_size * scales[pl.ds(slot, 1)])
        written(k).start()

    def only(k, act):
        if sources == chips:
            act()
        else:
            pl.when((chip ^ k) < sources)(act)

    for k in range(chips):
        only(k, functools.partial(update, k))
    for k in range(chips):
        only(k, lambda k=k: written(k).wait())


def weights(base, scales, momentum, blocks, filled=None, after=()):
    chips = len(blocks)
    slots, rows, cols = base.shape
    other = filled is not None
    ins = [(VMEM, value) for value in (base, scales, momentum, *blocks)]
    aliases = None
    if other:
        aliases = {len(ins): 0}
        ins.append((HBM, filled))
    (out,) = call(
        functools.partial(weight_kernel, chips, other, rows * chips * CORES),
        "update_weight",
        ins,
        [(HBM, base.shape, jnp.float32)],
        [
            pltpu.VMEM((chips, cols, cols), jnp.bfloat16),
            pltpu.VMEM((chips, rows, cols), jnp.float32),
            pltpu.SemaphoreType.DMA((chips,)),
        ],
        after,
        aliases,
    )
    return out


def merge_kernel(own, sibling, out, token, sem):
    token[...] = jnp.zeros_like(token)
    _, _, core = whereabouts()
    copies = []
    for s in range(own.shape[0]):
        for half, place in ((own, core), (sibling, 1 - core)):
            to = out.at[s * CORES + place]
            copies.append(pltpu.make_async_copy(half.at[s], to, sem.at[len(copies)]))
            copies[-1].start()
    for copy in copies:
        copy.wait()


def merge(own, sibling):
    sources, rows, cols = own.shape
    return call(
        merge_kernel,
        "merge_momentum",
        [(VMEM, own), (VMEM, sibling)],
        [(HBM, (sources * CORES, rows, cols), jnp.float32), (VMEM, (8, LEFT), jnp.float32)],
        [pltpu.SemaphoreType.DMA((sources * CORES,))],
    )


def key_kernel(peak, weight, out):
    owner, _, _ = whereabouts()
    heads_own, _, cols = weight.shape
    for i in range(heads_own):
        gamma = head_scale(peak, owner * heads_own + i, (1, cols))
        out[i] = weight[i] * jnp.sqrt(gamma)


def keys(peak, weight):
    (out,) = call(
        key_kernel,
        "scale_keys",
        [(SMEM, peak), (VMEM, weight)],
        [(VMEM, weight.shape, jnp.float32)],
    )
    return out


def body(grad_partials, assignment, momentum, q_weight, k_weight, max_logits):
    heads_own = grad_partials.shape[2]
    sources = lax.axis_size("owner")
    devices = lax.axis_size("dp") * lax.axis_size("context")
    chips = devices // CORES
    assignment = assignment.T

    def swap(value, bits):
        return lax.ppermute(value, PLANE, [(i, i ^ bits) for i in range(devices)])

    g = jnp.transpose(grad_partials[0], (1, 2, 0))
    if (g.shape[2] // chips) % 128:
        g = jnp.transpose(g.reshape(g.shape[:2] + (chips, g.shape[2] // chips)), (0, 2, 1, 3))
    order = list(range(sources))[::-1]
    size = max(1, sources // GROUPS)
    groups = [order[at : at + size] for at in range(0, sources, size)]
    first, token = fetch(assignment, g, [[(k, True) for k in groups[0]]])
    wanted = [[(k, True) for k in order[size:]], [(k, False) for k in groups[0]]]
    old, others, *own, _ = fetch(assignment, g, wanted, (momentum, max_logits), [token])
    siblings = [swap(first, 1)]

    near, arrived, before, sent = None, {}, [], []
    for i, ks in enumerate(groups):
        heads = [(j, j + (size * (i - 1) if i else 0)) for j in range(len(ks))]
        passed = [others, old] if i == 0 else []
        note = [peak] if i == len(groups) - 2 else []
        values = pair_sums(own[i], siblings[min(i, 1)], heads, chips, before, note, passed)
        here, away = values[0], values[1:chips]
        if i == 0:
            others, old = values[chips:]
            wanted = [[(k, False) for k in ks] for ks in groups[1:]]
            own += fetch(assignment, g, wanted, after=[away[0]])
            siblings.append(swap(others, 1))
            turned, peak = turn(momentum, swap(old, 1), max_logits)
        away = [swap(value, CORES * (k + 1)) for k, value in enumerate(away)]
        before = away[:2] if i else [away[0], turned]
        totals = list(plane_sums(here, away, [k == 0 for k in ks], sent, note))
        if note:
            peak = totals.pop()
            base, scales = bases(assignment, peak, q_weight, heads_own, k_weight.shape[2])
            k_weight_out = keys(peak, k_weight)
        sent = []
        for k, total in zip(ks, totals):
            if k == 0:
                near = total
            else:
                arrived[k] = lax.ppermute(total, "owner", [(j, j ^ k) for j in range(sources)])
                sent.append(arrived[k])
        if note:
            sent += [base, k_weight_out]

    arrived = [arrived[k] for k in range(1, sources)]
    new, here, *away = grams(assignment, turned, near, arrived, chips, heads_own, [])
    away = [swap(value, CORES * (k + 1)) for k, value in enumerate(away)]
    result = newton(here, away, momentum.shape[2], [])
    own_new, sibling_new = turn_back(new, [result])

    sibling_new = swap(sibling_new, 1)
    results = [result] + [swap(result, CORES * k) for k in range(1, chips)]
    sibling_results = [swap(value, 1) for value in results]
    momentum_out, token = merge(own_new, sibling_new)
    q_weight_out = weights(base, scales, own_new, results, after=[token])
    q_weight_out = weights(base, scales, sibling_new, sibling_results, q_weight_out)
    return (momentum_out, q_weight_out, k_weight_out)


def solution(mesh):
    rows = P("owner", ("dp", "context"), None)
    return jax.shard_map(
        body,
        mesh=mesh,
        in_specs=(
            P(("dp", "context"), None, "owner", None),
            P(),
            rows,
            rows,
            rows,
            P("context", None),
        ),
        out_specs=(rows, rows, rows),
        check_vma=False,
    )
```

```python
import functools
import math

import jax
import jax.numpy as jnp
from jax import lax
from jax.experimental import pallas as pl
from jax.experimental.pallas import tpu as pltpu
from jax.sharding import PartitionSpec as P

ITERS = 2
MOMENTUM_RATE = 0.95
WEIGHT_KEEP = 0.98
LOGIT_CAP = 100.0
QUINTIC_A = 3.4445
QUINTIC_B = -4.775
QUINTIC_C = 2.0315

CORES = 2
PLANE = ("dp", "context")
NORM_ROWS = 16
TILE = 16
LEVELS = 14.99
STEPS = 8.0
LOWEST = 100.0 * STEPS
NOTE_UNITS = (64.0, 64.0 * 32768.0, 64.0 * 32768.0 * 32768.0)
GROUPS = 4
LEFT = 128

SMEM = pl.BlockSpec(memory_space=pltpu.SMEM)
VMEM = pl.BlockSpec(memory_space=pltpu.VMEM)
ANY = pl.BlockSpec(memory_space=pl.ANY)
HBM = pl.BlockSpec(memory_space=pltpu.HBM)
PARAMS = pltpu.CompilerParams(vmem_limit_bytes=36 * 1024 * 1024)
FIRST = pltpu.CompilerParams(vmem_limit_bytes=52 * 1024 * 1024)
SECOND = pltpu.CompilerParams(vmem_limit_bytes=44 * 1024 * 1024)


def whereabouts():
    device = lax.axis_index("dp") * lax.axis_size("context") + lax.axis_index("context")
    return lax.axis_index("owner"), device // CORES, device % CORES


def call(kernel, name, ins, outs, scratch=(), after=(), aliases=None, params=PARAMS):
    count = len(ins)

    def whole(*refs):
        kernel(*refs[:count], *refs[count + len(after) :])

    return pl.pallas_call(
        whole,
        in_specs=[spec for spec, _ in ins] + [ANY] * len(after),
        out_specs=[spec for spec, _, _ in outs],
        out_shape=[jax.ShapeDtypeStruct(shape, dtype) for _, shape, dtype in outs],
        scratch_shapes=list(scratch),
        input_output_aliases=aliases or {},
        compiler_params=params,
        name=name,
    )(*[array for _, array in ins], *after)


def head_of(assignment, block, who, place, heads_own):
    found, seen = 0, 0
    for i in range(heads_own):
        hit = (assignment[0, block * heads_own + i] == who).astype(jnp.int32)
        found = jnp.where((hit == 1) & (seen == place), i, found)
        seen = seen + hit
    return found, seen


def bits_of(number):
    rows = jnp.broadcast_to(number.astype(jnp.int32), (TILE, number.shape[1]))
    return lax.shift_right_logical(rows, lax.broadcasted_iota(jnp.int32, rows.shape, 0)) & 1


def number_of(rows):
    bits = rows.astype(jnp.int32) & 1
    bits = lax.shift_left(bits, lax.broadcasted_iota(jnp.int32, bits.shape, 0))
    return jnp.sum(bits.astype(jnp.float32), axis=0, keepdims=True)


def encode(parts, out, note=None):
    top = functools.reduce(jnp.maximum, [jnp.max(jnp.abs(p), axis=0, keepdims=True) for p in parts])
    level = jnp.clip(jnp.ceil(STEPS * jnp.log2(top)), -LOWEST, 128.0 * STEPS)
    factor = jnp.exp2(LEVELS - level * (1.0 / STEPS))
    numbers = [level + LOWEST]
    if note is not None:
        rest = note * NOTE_UNITS[0]
        for _ in NOTE_UNITS:
            numbers.append(jnp.floor(rest))
            rest = (rest - numbers[-1]) * 32768.0
    at = 0
    for p in parts:
        coded = jnp.round(p * factor).astype(jnp.int32)
        if at == 0:
            head = len(numbers) * TILE
            tiles = [
                (coded[i * TILE : (i + 1) * TILE] & -2) | bits_of(number)
                for i, number in enumerate(numbers)
            ]
            for i, tile in enumerate(tiles):
                out[i * TILE : (i + 1) * TILE] = tile.astype(jnp.int16)
            out[head : p.shape[0]] = coded[head:].astype(jnp.int16)
        else:
            out[at : at + p.shape[0]] = coded.astype(jnp.int16)
        at += p.shape[0]


def noted(block, width):
    tiles = [block[i * TILE : (i + 1) * TILE] for i in range(1, 1 + len(NOTE_UNITS))]
    parts = [number_of(tile)[:, :width] / unit for tile, unit in zip(tiles, NOTE_UNITS)]
    return parts[0] + (parts[1] + parts[2])


def decode(block, count):
    size = block.shape[0] // count
    level = number_of(block[:TILE]) - LOWEST
    factor = jnp.exp2(level * (1.0 / STEPS) - LEVELS)
    return [
        block[i * size : (i + 1) * size].astype(jnp.int32).astype(jnp.float32) * factor
        for i in range(count)
    ]


def fetch_kernel(heads_own, wanted, assignment, g, *refs):
    owner, _, core = whereabouts()
    token, outs, sem = refs[-2], refs[:-2], refs[-1]
    if len(refs) > len(wanted) + 2:
        token, outs, sem, held, seen = refs[-4], refs[:-4], *refs[-3:]
    token[...] = jnp.zeros_like(token)
    copies = []
    for group, out in zip(wanted, outs[-len(wanted) :]):
        for i, (k, other) in enumerate(group):
            place = 1 - core if other else core
            head, _ = head_of(assignment, owner, owner ^ k, place, heads_own)
            copies.append(pltpu.make_async_copy(g.at[head], out.at[i], sem.at[len(copies)]))
            copies[-1].start()
    if len(outs) > len(wanted):
        momentum, logits, old = outs[:3]
        cols = momentum.shape[2]
        for s in range(old.shape[0]):
            copies.append(
                pltpu.make_async_copy(momentum.at[s * CORES + 1 - core], held.at[s], sem.at[len(copies)])
            )
            copies[-1].start()
        copies.append(pltpu.make_async_copy(logits, seen, sem.at[len(copies)]))
        copies[-1].start()
    for copy in copies:
        copy.wait()
    if len(outs) > len(wanted):
        old[:, :, :cols] = held[...]
        old[0, 0:1, cols : cols + logits.shape[1]] = seen[...]


def fetch(assignment, g, wanted, rest=(), after=()):
    outs = [(VMEM, (len(group),) + g.shape[1:], g.dtype) for group in wanted]
    count = sum(len(group) for group in wanted)
    ins = [(SMEM, assignment), (ANY, g)]
    outs.append((VMEM, (8, LEFT), jnp.float32))
    held = []
    if rest:
        momentum, logits = rest
        slots, rows, cols = momentum.shape
        outs = [(VMEM, (slots // CORES, rows, 2 * LEFT), momentum.dtype)] + outs
        ins += [(HBM, momentum), (HBM, logits)]
        count += slots // CORES + 1
        held = [
            pltpu.VMEM((slots // CORES, rows, cols), momentum.dtype),
            pltpu.VMEM(logits.shape, logits.dtype),
        ]
    return call(
        functools.partial(fetch_kernel, g.shape[0], wanted),
        "fetch_heads",
        ins,
        outs,
        [pltpu.SemaphoreType.DMA((count,))] + held,
        after,
        params=SECOND if after else FIRST,
    )


def pair_kernel(chips, aligned, heads, passed, own, sibling, *refs):
    _, chip, _ = whereabouts()
    note = None
    refs = refs[passed : len(refs) - passed] if passed else refs
    if len(refs) > chips:
        logits, padded = refs[0], refs[-1]
        padded[...] = jnp.zeros_like(padded)
        padded[:, : logits.shape[1]] = logits[...]
        note, refs = padded[...], refs[1:-1]
    here, away = refs[0], refs[1:]
    width = here.shape[-1]
    for k in range(chips):
        to = chip ^ k
        blocks = []
        for mine, theirs in heads:
            if aligned:
                rows = pl.ds(pl.multiple_of(to * width, 128), width)
                first, second = own[mine, :, rows], sibling[theirs, :, rows]
            else:
                first, second = own[mine, to], sibling[theirs, to]
            blocks.append(first.astype(jnp.float32) + second.astype(jnp.float32))
        if k == 0:
            for i, block in enumerate(blocks):
                here[i] = block
        else:
            encode(blocks, away[k - 1], note if k == 1 else None)


def pair_sums(own, sibling, heads, chips, after, note, passed):
    aligned = own.ndim == 3
    cols = own.shape[-2]
    width = own.shape[-1] // chips if aligned else own.shape[-1]
    coded = (VMEM, (len(heads) * cols, width), jnp.int16)
    outs = [(VMEM, (len(heads), cols, width), jnp.float32)] + [coded] * (chips - 1)
    return call(
        functools.partial(pair_kernel, chips, aligned, heads, len(passed)),
        "pair_sum",
        [(VMEM, own), (VMEM, sibling)]
        + [(ANY, value) for value in passed]
        + [(VMEM, value) for value in note],
        outs + [(ANY, value.shape, value.dtype) for value in passed],
        [pltpu.VMEM((1, width), jnp.float32) for _ in note],
        after=after,
        aliases={2 + i: chips + i for i in range(len(passed))},
    )


def plane_kernel(plain, noting, here, *refs):
    outs = refs[-len(plain) - noting :]
    away = refs[: len(refs) - len(outs)]
    if noting:
        logits, away = away[-1], away[:-1]
        peak, outs = outs[-1], outs[:-1]
        peak[...] = jnp.maximum(logits[...], noted(away[0], logits.shape[1]))
    blocks = [here[i] for i in range(len(plain))]
    for value in away:
        blocks = [a + b for a, b in zip(blocks, decode(value, len(plain)))]
    for is_plain, block, out in zip(plain, blocks, outs):
        if is_plain:
            out[...] = block
        else:
            encode([block], out)


def plane_sums(here, away, plain, after, note):
    _, cols, width = here.shape
    coded = (VMEM, (cols, width), jnp.int16)
    outs = [(VMEM, (cols, width), jnp.float32) if p else coded for p in plain]
    return call(
        functools.partial(plane_kernel, plain, len(note)),
        "plane_sum",
        [(VMEM, value) for value in (here, *away, *note)],
        outs + [(VMEM, value.shape, value.dtype) for value in note],
        after=after,
    )


def turn_kernel(own, sibling, logits, out, peak, both):
    _, _, core = whereabouts()
    rows = own.shape[1]
    for s in range(sibling.shape[0]):
        both[pl.ds(pl.multiple_of(core * rows, 16), rows)] = own[s * CORES + core]
        both[pl.ds(pl.multiple_of((1 - core) * rows, 16), rows)] = sibling[s, :, : own.shape[2]]
        out[s] = both[...].T
    cols = own.shape[2]
    peak[...] = jnp.maximum(logits[...], sibling[0, 0:1, cols : cols + logits.shape[1]])


def turn(own, sibling, logits):
    sources = sibling.shape[0]
    _, rows, cols = own.shape
    return call(
        turn_kernel,
        "turn_momentum",
        [(VMEM, own), (VMEM, sibling), (VMEM, logits)],
        [(VMEM, (sources, cols, CORES * rows), jnp.float32), (VMEM, logits.shape, logits.dtype)],
        [pltpu.VMEM((CORES * rows, cols), jnp.float32)],
    )


def pack(matrix, out):
    cols = matrix.shape[0]
    rest = cols - LEFT
    out[:cols] = matrix[:, :LEFT].astype(out.dtype)
    for f in range(2):
        part = matrix[LEFT + f * rest // 2 : LEFT + (f + 1) * rest // 2, LEFT:]
        out[cols : cols + rest // 2, f * rest : (f + 1) * rest] = part.astype(out.dtype)


def unpack(packed, out):
    cols = out.shape[0]
    rest = cols - LEFT
    out[:, :LEFT] = packed[:cols]
    out[:LEFT, LEFT:] = packed[LEFT:cols].astype(jnp.float32).T.astype(out.dtype)
    for f in range(2):
        part = packed[cols : cols + rest // 2, f * rest : (f + 1) * rest]
        out[LEFT + f * rest // 2 : LEFT + (f + 1) * rest // 2, LEFT:] = part


def gram_kernel(chips, heads_own, assignment, old, near, *refs):
    sources = old.shape[0]
    arrived, refs = refs[: sources - 1], refs[sources - 1 :]
    (new, here), away, packed = refs[:2], refs[2:-1], refs[-1]
    owner, chip, core = whereabouts()
    for k in range(sources):
        source = owner ^ k
        grad = near[...] if k == 0 else decode(arrived[k - 1], 1)[0]
        kept = old[source]
        _, held = head_of(assignment, source, owner, 0, heads_own)
        new[source] = jnp.where(held > core, MOMENTUM_RATE * kept + grad, kept)
    for k in range(chips):
        value = new[lax.rem(chip ^ k, sources)].astype(jnp.bfloat16)
        gram = lax.dot_general(
            value, value, (((1,), (1,)), ((), ())), preferred_element_type=jnp.float32
        )
        if k == 0:
            pack(gram, here)
        else:
            pack(gram, packed)
            encode([packed[...]], away[k - 1])


def grams(assignment, old, near, arrived, chips, heads_own, after):
    cols = old.shape[1]
    rows = cols + (cols - LEFT) // 2
    coded = (VMEM, (rows, LEFT), jnp.int16)
    return call(
        functools.partial(gram_kernel, chips, heads_own),
        "refresh_and_gram",
        [(SMEM, assignment)] + [(VMEM, value) for value in (old, near, *arrived)],
        [(VMEM, old.shape, jnp.float32), (VMEM, (rows, LEFT), jnp.float32)] + [coded] * (chips - 1),
        [pltpu.VMEM((rows, LEFT), jnp.float32)],
        after,
    )


def small_dot(a, b):
    return lax.dot_general(
        a.astype(jnp.bfloat16), b.astype(jnp.bfloat16), (((1,), (0,)), ((), ())),
        preferred_element_type=jnp.float32,
    )


def newton_kernel(here, *refs):
    away, (out, square) = refs[:-2], refs[-2:]
    cols = square.shape[0]
    total = here[...]
    for block in away:
        total = total + decode(block, 1)[0]
    unpack(total, square)
    gram = square[...]
    row = lax.broadcasted_iota(jnp.int32, gram.shape, 0)
    column = lax.broadcasted_iota(jnp.int32, gram.shape, 1)
    square_sum = jnp.sum(jnp.where(row == column, gram, 0.0), axis=(0, 1), keepdims=True)
    norm = jnp.sqrt(square_sum) + 1e-07
    inverse = 1.0 / norm
    gram = jnp.where(norm < jnp.inf, gram * inverse * inverse, 0.0)
    first = QUINTIC_B * gram + QUINTIC_C * small_dot(gram, gram)
    twice = (2.0 * QUINTIC_A) * first + small_dot(first, first)
    gram = (QUINTIC_A * QUINTIC_A) * gram + small_dot(gram, twice)
    second = QUINTIC_B * gram + QUINTIC_C * small_dot(gram, gram)
    result = QUINTIC_A * (first + second) + small_dot(first, second)
    pack(result, out)
    high = norm.astype(jnp.bfloat16).astype(jnp.float32)
    middle = (norm - high).astype(jnp.bfloat16).astype(jnp.float32)
    low = norm - high - middle
    row = lax.broadcasted_iota(jnp.int32, (NORM_ROWS, LEFT), 0)
    scales = jnp.where(row == 0, high, jnp.where(row == 1, middle, jnp.where(row == 2, low, 0.0)))
    out[out.shape[0] - NORM_ROWS :] = scales.astype(jnp.bfloat16)


def newton(here, away, cols, after):
    (out,) = call(
        newton_kernel,
        "newton_schulz",
        [(VMEM, value) for value in (here, *away)],
        [(VMEM, (here.shape[0] + NORM_ROWS, LEFT), jnp.bfloat16)],
        [pltpu.VMEM((cols, cols), jnp.float32)],
        after,
    )
    return out


def back_kernel(new, own, sibling, both):
    _, _, core = whereabouts()
    rows = own.shape[1]
    for s in range(own.shape[0]):
        both[...] = new[s].T
        own[s] = both[pl.ds(pl.multiple_of(core * rows, 16), rows)]
        sibling[s] = both[pl.ds(pl.multiple_of((1 - core) * rows, 16), rows)]


def turn_back(new, after):
    sources, cols, width = new.shape
    half = (VMEM, (sources, width // CORES, cols), jnp.float32)
    return call(
        back_kernel,
        "turn_back",
        [(VMEM, new)],
        [half, half],
        [pltpu.VMEM((width, cols), jnp.float32)],
        after,
    )


def head_scale(peak, head, shape):
    return jnp.minimum(1.0, LOGIT_CAP / jnp.full(shape, peak[0, head], jnp.float32))


def base_kernel(heads_own, kn_count, assignment, peak, weight, out, scales):
    owner, _, _ = whereabouts()
    slots, _, cols = weight.shape
    column = lax.broadcasted_iota(jnp.int32, (1, cols), 1)
    for slot in range(slots):
        source, place = slot // CORES, slot % CORES
        head, held = head_of(assignment, source, owner, place, heads_own)
        gamma = head_scale(peak, source * heads_own + head, (1, cols))
        scale = jnp.where(column < kn_count, jnp.sqrt(gamma), gamma)
        old = weight[slot]
        out[slot] = jnp.where(held > place, (WEIGHT_KEEP * old) * scale, old)
        scales[slot : slot + 1] = jnp.where(held > place, scale, 0.0)


def bases(assignment, peak, weight, heads_own, kn_count):
    slots, _, cols = weight.shape
    return call(
        functools.partial(base_kernel, heads_own, kn_count),
        "scale_weight",
        [(SMEM, assignment), (SMEM, peak), (VMEM, weight)],
        [(VMEM, weight.shape, jnp.float32), (VMEM, (slots, cols), jnp.float32)],
    )


def weight_kernel(chips, other, rows_all, base, scales, momentum, *refs):
    blocks, refs = refs[:chips], refs[chips:]
    out, momentum_out, matrix, result, sem, momentum_sem = refs[-6:]
    slots, _, cols = base.shape
    sources = slots // CORES
    step_size = 0.04 * math.sqrt(max(rows_all, cols))
    _, chip, core = whereabouts()
    place = 1 - core if other else core
    def stored(s):
        to = momentum_out.at[s * CORES + place]
        return pltpu.make_async_copy(momentum.at[s], to, momentum_sem.at[s])

    for s in range(sources):
        stored(s).start()

    def written(k):
        return pltpu.make_async_copy(result.at[k], out.at[(chip ^ k) * CORES + place], sem.at[k])

    def update(k):
        source = chip ^ k
        slot = source * CORES + place
        block = blocks[k]
        parts = block[block.shape[0] - NORM_ROWS :].astype(jnp.float32)
        norm = parts[0:1, 0:1] + parts[1:2, 0:1] + parts[2:3, 0:1]
        unpack(block[: block.shape[0] - NORM_ROWS], matrix.at[k])
        start = (momentum[source] * (1.0 / norm)).astype(jnp.bfloat16)
        step = (QUINTIC_A * QUINTIC_A) * start.astype(jnp.float32) + small_dot(start, matrix[k])
        result[k] = base[slot] - step * (step_size * scales[pl.ds(slot, 1)])
        written(k).start()

    def only(k, act):
        if sources == chips:
            act()
        else:
            pl.when((chip ^ k) < sources)(act)

    for k in range(chips):
        only(k, functools.partial(update, k))
    for k in range(chips):
        only(k, lambda k=k: written(k).wait())
    for s in range(sources):
        stored(s).wait()


def weights(base, scales, momentum, blocks, filled=()):
    chips = len(blocks)
    slots, rows, cols = base.shape
    ins = [(VMEM, value) for value in (base, scales, momentum, *blocks)]
    aliases = {len(ins) + i: i for i in range(len(filled))}
    return call(
        functools.partial(weight_kernel, chips, bool(filled), rows * chips * CORES),
        "update_weight",
        ins + [(HBM, value) for value in filled],
        [(HBM, base.shape, jnp.float32)] * 2,
        [
            pltpu.VMEM((chips, cols, cols), jnp.bfloat16),
            pltpu.VMEM((chips, rows, cols), jnp.float32),
            pltpu.SemaphoreType.DMA((chips,)),
            pltpu.SemaphoreType.DMA((slots // CORES,)),
        ],
        aliases=aliases,
    )


def key_kernel(peak, weight, out):
    owner, _, _ = whereabouts()
    heads_own, _, cols = weight.shape
    for i in range(heads_own):
        gamma = head_scale(peak, owner * heads_own + i, (1, cols))
        out[i] = weight[i] * jnp.sqrt(gamma)


def keys(peak, weight):
    (out,) = call(
        key_kernel,
        "scale_keys",
        [(SMEM, peak), (VMEM, weight)],
        [(VMEM, weight.shape, jnp.float32)],
    )
    return out


def body(grad_partials, assignment, momentum, q_weight, k_weight, max_logits):
    heads_own = grad_partials.shape[2]
    sources = lax.axis_size("owner")
    devices = lax.axis_size("dp") * lax.axis_size("context")
    chips = devices // CORES
    assignment = assignment.T

    def swap(value, bits):
        return lax.ppermute(value, PLANE, [(i, i ^ bits) for i in range(devices)])

    g = jnp.transpose(grad_partials[0], (1, 2, 0))
    if (g.shape[2] // chips) % 128:
        g = jnp.transpose(g.reshape(g.shape[:2] + (chips, g.shape[2] // chips)), (0, 2, 1, 3))
    order = list(range(sources))[::-1]
    size = max(1, sources // GROUPS)
    groups = [order[at : at + size] for at in range(0, sources, size)]
    old, first, token = fetch(assignment, g, [[(k, True) for k in groups[0]]], (momentum, max_logits))
    wanted = [[(k, True) for k in order[size:]], [(k, False) for k in groups[0]]]
    others, *own, _ = fetch(assignment, g, wanted, after=[token])
    siblings = [swap(first, 1)]

    near, arrived, before, sent = None, {}, [], []
    for i, ks in enumerate(groups):
        heads = [(j, j + (size * (i - 1) if i else 0)) for j in range(len(ks))]
        passed = [others] if i == 0 else []
        note = [peak] if i == len(groups) - 2 else []
        values = pair_sums(own[i], siblings[min(i, 1)], heads, chips, before, note, passed)
        here, away = values[0], values[1:chips]
        if i == 0:
            siblings.append(swap(values[chips], 1))
            turned, peak = turn(momentum, swap(old, 1), max_logits)
            wanted = [[(k, False) for k in ks] for ks in groups[1:]]
            *own[1:], _ = fetch(assignment, g, wanted, after=[away[0]])
        away = [swap(value, CORES * (k + 1)) for k, value in enumerate(away)]
        before = away[:2] if i else [away[0], turned]
        totals = list(plane_sums(here, away, [k == 0 for k in ks], sent, note))
        if note:
            peak = totals.pop()
            base, scales = bases(assignment, peak, q_weight, heads_own, k_weight.shape[2])
            k_weight_out = keys(peak, k_weight)
        sent = []
        for k, total in zip(ks, totals):
            if k == 0:
                near = total
            else:
                arrived[k] = lax.ppermute(total, "owner", [(j, j ^ k) for j in range(sources)])
                sent.append(arrived[k])
        if note:
            sent += [base, k_weight_out]

    arrived = [arrived[k] for k in range(1, sources)]
    new, here, *away = grams(assignment, turned, near, arrived, chips, heads_own, [])
    away = [swap(value, CORES * (k + 1)) for k, value in enumerate(away)]
    result = newton(here, away[::-1], momentum.shape[2], [])
    own_new, sibling_new = turn_back(new, [result])

    sibling_new = swap(sibling_new, 1)
    results = [result] + [swap(result, CORES * k) for k in range(1, chips)]
    sibling_results = [swap(value, 1) for value in results]
    filled = weights(base, scales, own_new, results)
    q_weight_out, momentum_out = weights(base, scales, sibling_new, sibling_results, filled)
    return (momentum_out, q_weight_out, k_weight_out)


def solution(mesh):
    rows = P("owner", ("dp", "context"), None)
    return jax.shard_map(
        body,
        mesh=mesh,
        in_specs=(
            P(("dp", "context"), None, "owner", None),
            P(),
            rows,
            rows,
            rows,
            P("context", None),
        ),
        out_specs=(rows, rows, rows),
        check_vma=False,
    )
```

```python
import functools
import math

import jax
import jax.numpy as jnp
from jax import lax
from jax.experimental import pallas as pl
from jax.experimental.pallas import tpu as pltpu
from jax.sharding import PartitionSpec as P

ITERS = 2
MOMENTUM_RATE = 0.95
WEIGHT_KEEP = 0.98
LOGIT_CAP = 100.0
QUINTIC_A = 3.4445
QUINTIC_B = -4.775
QUINTIC_C = 2.0315

CORES = 2
PLANE = ("dp", "context")
NORM_ROWS = 16
TILE = 16
LEVELS = 14.99
STEPS = 8.0
LOWEST = 100.0 * STEPS
NOTE_UNITS = (64.0, 64.0 * 32768.0, 64.0 * 32768.0 * 32768.0)
GROUPS = 4
TOGETHER = 2
LEFT = 128

SMEM = pl.BlockSpec(memory_space=pltpu.SMEM)
VMEM = pl.BlockSpec(memory_space=pltpu.VMEM)
ANY = pl.BlockSpec(memory_space=pl.ANY)
HBM = pl.BlockSpec(memory_space=pltpu.HBM)
PARAMS = pltpu.CompilerParams(vmem_limit_bytes=36 * 1024 * 1024)
FIRST = pltpu.CompilerParams(vmem_limit_bytes=52 * 1024 * 1024)
SECOND = pltpu.CompilerParams(vmem_limit_bytes=44 * 1024 * 1024)


def whereabouts():
    device = lax.axis_index("dp") * lax.axis_size("context") + lax.axis_index("context")
    return lax.axis_index("owner"), device // CORES, device % CORES


def call(kernel, name, ins, outs, scratch=(), after=(), aliases=None, params=PARAMS):
    count = len(ins)

    def whole(*refs):
        kernel(*refs[:count], *refs[count + len(after) :])

    return pl.pallas_call(
        whole,
        in_specs=[spec for spec, _ in ins] + [ANY] * len(after),
        out_specs=[spec for spec, _, _ in outs],
        out_shape=[jax.ShapeDtypeStruct(shape, dtype) for _, shape, dtype in outs],
        scratch_shapes=list(scratch),
        input_output_aliases=aliases or {},
        compiler_params=params,
        name=name,
    )(*[array for _, array in ins], *after)


def head_of(assignment, block, who, place, heads_own):
    found, seen = 0, 0
    for i in range(heads_own):
        hit = (assignment[0, block * heads_own + i] == who).astype(jnp.int32)
        found = jnp.where((hit == 1) & (seen == place), i, found)
        seen = seen + hit
    return found, seen


def bits_of(number):
    rows = jnp.broadcast_to(number.astype(jnp.int32), (TILE, number.shape[1]))
    return lax.shift_right_logical(rows, lax.broadcasted_iota(jnp.int32, rows.shape, 0)) & 1


def number_of(rows):
    bits = rows.astype(jnp.int32) & 1
    bits = lax.shift_left(bits, lax.broadcasted_iota(jnp.int32, bits.shape, 0))
    return jnp.sum(bits.astype(jnp.float32), axis=0, keepdims=True)


def encode(parts, out, note=None):
    top = functools.reduce(jnp.maximum, [jnp.max(jnp.abs(p), axis=0, keepdims=True) for p in parts])
    level = jnp.clip(jnp.ceil(STEPS * jnp.log2(top)), -LOWEST, 128.0 * STEPS)
    factor = jnp.exp2(LEVELS - level * (1.0 / STEPS))
    numbers = [level + LOWEST]
    if note is not None:
        rest = note * NOTE_UNITS[0]
        for _ in NOTE_UNITS:
            numbers.append(jnp.floor(rest))
            rest = (rest - numbers[-1]) * 32768.0
    at = 0
    for p in parts:
        coded = jnp.round(p * factor).astype(jnp.int32)
        if at == 0:
            head = len(numbers) * TILE
            tiles = [
                (coded[i * TILE : (i + 1) * TILE] & -2) | bits_of(number)
                for i, number in enumerate(numbers)
            ]
            for i, tile in enumerate(tiles):
                out[i * TILE : (i + 1) * TILE] = tile.astype(jnp.int16)
            out[head : p.shape[0]] = coded[head:].astype(jnp.int16)
        else:
            out[at : at + p.shape[0]] = coded.astype(jnp.int16)
        at += p.shape[0]


def noted(block, width):
    tiles = [block[i * TILE : (i + 1) * TILE] for i in range(1, 1 + len(NOTE_UNITS))]
    parts = [number_of(tile)[:, :width] / unit for tile, unit in zip(tiles, NOTE_UNITS)]
    return parts[0] + (parts[1] + parts[2])


def decode(block, count):
    size = block.shape[0] // count
    level = number_of(block[:TILE]) - LOWEST
    factor = jnp.exp2(level * (1.0 / STEPS) - LEVELS)
    return [
        block[i * size : (i + 1) * size].astype(jnp.int32).astype(jnp.float32) * factor
        for i in range(count)
    ]


def fetch_kernel(heads_own, wanted, assignment, g, *refs):
    owner, _, core = whereabouts()
    token, outs, sem = refs[-2], refs[:-2], refs[-1]
    if len(refs) > len(wanted) + 2:
        token, outs, sem, held, seen = refs[-4], refs[:-4], *refs[-3:]
    token[...] = jnp.zeros_like(token)
    copies = []
    for group, out in zip(wanted, outs[-len(wanted) :]):
        for i, (k, other) in enumerate(group):
            place = 1 - core if other else core
            head, _ = head_of(assignment, owner, owner ^ k, place, heads_own)
            copies.append(pltpu.make_async_copy(g.at[head], out.at[i], sem.at[len(copies)]))
            copies[-1].start()
    if len(outs) > len(wanted):
        momentum, logits, old = outs[:3]
        cols = momentum.shape[2]
        for s in range(old.shape[0]):
            copies.append(
                pltpu.make_async_copy(momentum.at[s * CORES + 1 - core], held.at[s], sem.at[len(copies)])
            )
            copies[-1].start()
        copies.append(pltpu.make_async_copy(logits, seen, sem.at[len(copies)]))
        copies[-1].start()
    for copy in copies:
        copy.wait()
    if len(outs) > len(wanted):
        old[:, :, :cols] = held[...]
        old[0, 0:1, cols : cols + logits.shape[1]] = seen[...]


def fetch(assignment, g, wanted, rest=(), after=()):
    outs = [(VMEM, (len(group),) + g.shape[1:], g.dtype) for group in wanted]
    count = sum(len(group) for group in wanted)
    ins = [(SMEM, assignment), (ANY, g)]
    outs.append((VMEM, (8, LEFT), jnp.float32))
    held = []
    if rest:
        momentum, logits = rest
        slots, rows, cols = momentum.shape
        outs = [(VMEM, (slots // CORES, rows, 2 * LEFT), momentum.dtype)] + outs
        ins += [(HBM, momentum), (HBM, logits)]
        count += slots // CORES + 1
        held = [
            pltpu.VMEM((slots // CORES, rows, cols), momentum.dtype),
            pltpu.VMEM(logits.shape, logits.dtype),
        ]
    return call(
        functools.partial(fetch_kernel, g.shape[0], wanted),
        "fetch_heads",
        ins,
        outs,
        [pltpu.SemaphoreType.DMA((count,))] + held,
        after,
        params=SECOND if after else FIRST,
    )


def pair_kernel(chips, aligned, heads, passed, own, sibling, *refs):
    _, chip, _ = whereabouts()
    note = None
    refs = refs[passed : len(refs) - passed] if passed else refs
    if len(refs) > chips:
        logits, padded = refs[0], refs[-1]
        padded[...] = jnp.zeros_like(padded)
        padded[:, : logits.shape[1]] = logits[...]
        note, refs = padded[...], refs[1:-1]
    here, away = refs[0], refs[1:]
    width = here.shape[-1]
    for k in range(chips):
        to = chip ^ k
        blocks = []
        for mine, theirs in heads:
            if aligned:
                rows = pl.ds(pl.multiple_of(to * width, 128), width)
                first, second = own[mine, :, rows], sibling[theirs, :, rows]
            else:
                first, second = own[mine, to], sibling[theirs, to]
            blocks.append(first.astype(jnp.float32) + second.astype(jnp.float32))
        if k == 0:
            for i, block in enumerate(blocks):
                here[i] = block
        else:
            encode(blocks, away[k - 1], note if k == 1 else None)


def pair_sums(own, sibling, heads, chips, after, note, passed):
    aligned = own.ndim == 3
    cols = own.shape[-2]
    width = own.shape[-1] // chips if aligned else own.shape[-1]
    coded = (VMEM, (len(heads) * cols, width), jnp.int16)
    outs = [(VMEM, (len(heads), cols, width), jnp.float32)] + [coded] * (chips - 1)
    return call(
        functools.partial(pair_kernel, chips, aligned, heads, len(passed)),
        "pair_sum",
        [(VMEM, own), (VMEM, sibling)]
        + [(ANY, value) for value in passed]
        + [(VMEM, value) for value in note],
        outs + [(ANY, value.shape, value.dtype) for value in passed],
        [pltpu.VMEM((1, width), jnp.float32) for _ in note],
        after=after,
        aliases={2 + i: chips + i for i in range(len(passed))},
    )


def plane_kernel(plain, noting, here, *refs):
    outs = refs[-len(plain) - noting :]
    away = refs[: len(refs) - len(outs)]
    if noting:
        logits, away = away[-1], away[:-1]
        peak, outs = outs[-1], outs[:-1]
        peak[...] = jnp.maximum(logits[...], noted(away[0], logits.shape[1]))
    blocks = [here[i] for i in range(len(plain))]
    for value in away:
        blocks = [a + b for a, b in zip(blocks, decode(value, len(plain)))]
    for is_plain, block, out in zip(plain, blocks, outs):
        if is_plain:
            out[...] = block
        else:
            encode([block], out)


def plane_sums(here, away, plain, after, note):
    _, cols, width = here.shape
    coded = (VMEM, (cols, width), jnp.int16)
    outs = [(VMEM, (cols, width), jnp.float32) if p else coded for p in plain]
    return call(
        functools.partial(plane_kernel, plain, len(note)),
        "plane_sum",
        [(VMEM, value) for value in (here, *away, *note)],
        outs + [(VMEM, value.shape, value.dtype) for value in note],
        after=after,
    )


def turn_kernel(own, sibling, logits, out, peak, both):
    _, _, core = whereabouts()
    rows = own.shape[1]
    for s in range(sibling.shape[0]):
        both[pl.ds(pl.multiple_of(core * rows, 16), rows)] = own[s * CORES + core]
        both[pl.ds(pl.multiple_of((1 - core) * rows, 16), rows)] = sibling[s, :, : own.shape[2]]
        out[s] = both[...].T
    cols = own.shape[2]
    peak[...] = jnp.maximum(logits[...], sibling[0, 0:1, cols : cols + logits.shape[1]])


def turn(own, sibling, logits):
    sources = sibling.shape[0]
    _, rows, cols = own.shape
    return call(
        turn_kernel,
        "turn_momentum",
        [(VMEM, own), (VMEM, sibling), (VMEM, logits)],
        [(VMEM, (sources, cols, CORES * rows), jnp.float32), (VMEM, logits.shape, logits.dtype)],
        [pltpu.VMEM((CORES * rows, cols), jnp.float32)],
    )


def pack(matrix, out):
    cols = matrix.shape[0]
    rest = cols - LEFT
    out[:cols] = matrix[:, :LEFT].astype(out.dtype)
    for f in range(2):
        part = matrix[LEFT + f * rest // 2 : LEFT + (f + 1) * rest // 2, LEFT:]
        out[cols : cols + rest // 2, f * rest : (f + 1) * rest] = part.astype(out.dtype)


def unpack(packed, out):
    cols = out.shape[0]
    rest = cols - LEFT
    out[:, :LEFT] = packed[:cols]
    out[:LEFT, LEFT:] = packed[LEFT:cols].astype(jnp.float32).T.astype(out.dtype)
    for f in range(2):
        part = packed[cols : cols + rest // 2, f * rest : (f + 1) * rest]
        out[LEFT + f * rest // 2 : LEFT + (f + 1) * rest // 2, LEFT:] = part


def refreshed(heads_own, assignment, old, grad, k):
    owner, _, core = whereabouts()
    source = owner ^ k
    _, held = head_of(assignment, source, owner, 0, heads_own)
    kept = old[source]
    return source, jnp.where(held > core, MOMENTUM_RATE * kept + grad, kept)


def gram_of(value, packed, coded):
    value = value.astype(jnp.bfloat16)
    gram = lax.dot_general(
        value, value, (((1,), (1,)), ((), ())), preferred_element_type=jnp.float32
    )
    pack(gram, packed)
    encode([packed[...]], coded)


def early_kernel(heads_own, ks, assignment, old, *refs):
    arrived, (new, packed, coded) = refs[: len(ks)], refs[len(ks) :]
    for i, k in enumerate(ks):
        _, new[i] = refreshed(heads_own, assignment, old, decode(arrived[i], 1)[0], k)
        gram_of(new[i], packed.at[i], coded.at[i])


def early_grams(assignment, old, arrived, ks, heads_own):
    _, cols, width = old.shape
    rows = cols + (cols - LEFT) // 2
    return call(
        functools.partial(early_kernel, heads_own, ks),
        "early_gram",
        [(SMEM, assignment)] + [(VMEM, value) for value in (old, *arrived)],
        [
            (VMEM, (len(ks), cols, width), jnp.float32),
            (VMEM, (len(ks), rows, LEFT), jnp.float32),
            (VMEM, (len(ks), rows, LEFT), jnp.int16),
        ],
    )


def gram_kernel(chips, heads_own, assignment, old, near, early_new, early_packed, early_coded, *refs):
    sources, count = old.shape[0], early_new.shape[0]
    late = sources - count
    arrived, refs = refs[: late - 1], refs[late - 1 :]
    (new, here), away, (packed, coded) = refs[:2], refs[2:-2], refs[-2:]
    owner, chip, _ = whereabouts()
    for k in range(late):
        grad = near[...] if k == 0 else decode(arrived[k - 1], 1)[0]
        source, value = refreshed(heads_own, assignment, old, grad, k)
        new[source] = value
        gram_of(value, packed.at[k], coded.at[k])
    for i in range(count):
        new[owner ^ (sources - 1 - i)] = early_new[i]
    for c in range(chips):
        k = lax.rem(chip ^ c, sources) ^ owner

        def from_early(c=c, k=k):
            if c == 0:
                here[...] = early_packed[sources - 1 - k]
            else:
                away[c - 1][...] = early_coded[sources - 1 - k]

        def from_late(c=c, k=k):
            if c == 0:
                here[...] = packed[k]
            else:
                away[c - 1][...] = coded[k]

        pl.when(k >= late)(from_early)
        pl.when(k < late)(from_late)


def grams(assignment, old, near, early, arrived, chips, heads_own, after):
    sources, cols, _ = old.shape
    rows = cols + (cols - LEFT) // 2
    late = sources - early[0].shape[0]
    coded = (VMEM, (rows, LEFT), jnp.int16)
    return call(
        functools.partial(gram_kernel, chips, heads_own),
        "refresh_and_gram",
        [(SMEM, assignment)] + [(VMEM, value) for value in (old, near, *early, *arrived)],
        [(VMEM, old.shape, jnp.float32), (VMEM, (rows, LEFT), jnp.float32)] + [coded] * (chips - 1),
        [pltpu.VMEM((late, rows, LEFT), jnp.float32), pltpu.VMEM((late, rows, LEFT), jnp.int16)],
        after,
    )


def small_dot(a, b):
    return lax.dot_general(
        a.astype(jnp.bfloat16), b.astype(jnp.bfloat16), (((1,), (0,)), ((), ())),
        preferred_element_type=jnp.float32,
    )


def newton_kernel(here, *refs):
    away, (out, square) = refs[:-2], refs[-2:]
    cols = square.shape[0]
    total = here[...]
    for block in away:
        total = total + decode(block, 1)[0]
    unpack(total, square)
    gram = square[...]
    row = lax.broadcasted_iota(jnp.int32, gram.shape, 0)
    column = lax.broadcasted_iota(jnp.int32, gram.shape, 1)
    square_sum = jnp.sum(jnp.where(row == column, gram, 0.0), axis=(0, 1), keepdims=True)
    norm = jnp.sqrt(square_sum) + 1e-07
    inverse = 1.0 / norm
    gram = jnp.where(norm < jnp.inf, gram * inverse * inverse, 0.0)
    first = QUINTIC_B * gram + QUINTIC_C * small_dot(gram, gram)
    twice = (2.0 * QUINTIC_A) * first + small_dot(first, first)
    gram = (QUINTIC_A * QUINTIC_A) * gram + small_dot(gram, twice)
    second = QUINTIC_B * gram + QUINTIC_C * small_dot(gram, gram)
    result = QUINTIC_A * (first + second) + small_dot(first, second)
    pack(result, out)
    high = norm.astype(jnp.bfloat16).astype(jnp.float32)
    middle = (norm - high).astype(jnp.bfloat16).astype(jnp.float32)
    low = norm - high - middle
    row = lax.broadcasted_iota(jnp.int32, (NORM_ROWS, LEFT), 0)
    scales = jnp.where(row == 0, high, jnp.where(row == 1, middle, jnp.where(row == 2, low, 0.0)))
    out[out.shape[0] - NORM_ROWS :] = scales.astype(jnp.bfloat16)


def newton(here, away, cols, after):
    (out,) = call(
        newton_kernel,
        "newton_schulz",
        [(VMEM, value) for value in (here, *away)],
        [(VMEM, (here.shape[0] + NORM_ROWS, LEFT), jnp.bfloat16)],
        [pltpu.VMEM((cols, cols), jnp.float32)],
        after,
    )
    return out


def back_kernel(new, own, sibling, both):
    _, _, core = whereabouts()
    rows = own.shape[1]
    for s in range(own.shape[0]):
        both[...] = new[s].T
        own[s] = both[pl.ds(pl.multiple_of(core * rows, 16), rows)]
        sibling[s] = both[pl.ds(pl.multiple_of((1 - core) * rows, 16), rows)]


def turn_back(new, after):
    sources, cols, width = new.shape
    half = (VMEM, (sources, width // CORES, cols), jnp.float32)
    return call(
        back_kernel,
        "turn_back",
        [(VMEM, new)],
        [half, half],
        [pltpu.VMEM((width, cols), jnp.float32)],
        after,
    )


def head_scale(peak, head, shape):
    return jnp.minimum(1.0, LOGIT_CAP / jnp.full(shape, peak[0, head], jnp.float32))


def base_kernel(heads_own, kn_count, assignment, peak, weight, out, scales):
    owner, _, _ = whereabouts()
    slots, _, cols = weight.shape
    column = lax.broadcasted_iota(jnp.int32, (1, cols), 1)
    for slot in range(slots):
        source, place = slot // CORES, slot % CORES
        head, held = head_of(assignment, source, owner, place, heads_own)
        gamma = head_scale(peak, source * heads_own + head, (1, cols))
        scale = jnp.where(column < kn_count, jnp.sqrt(gamma), gamma)
        old = weight[slot]
        out[slot] = jnp.where(held > place, (WEIGHT_KEEP * old) * scale, old)
        scales[slot : slot + 1] = jnp.where(held > place, scale, 0.0)


def bases(assignment, peak, weight, heads_own, kn_count):
    slots, _, cols = weight.shape
    return call(
        functools.partial(base_kernel, heads_own, kn_count),
        "scale_weight",
        [(SMEM, assignment), (SMEM, peak), (VMEM, weight)],
        [(VMEM, weight.shape, jnp.float32), (VMEM, (slots, cols), jnp.float32)],
    )


def weight_kernel(chips, other, rows_all, base, scales, momentum, *refs):
    blocks, refs = refs[:chips], refs[chips:]
    out, momentum_out, matrix, result, sem, momentum_sem = refs[-6:]
    slots, _, cols = base.shape
    sources = slots // CORES
    step_size = 0.04 * math.sqrt(max(rows_all, cols))
    _, chip, core = whereabouts()
    place = 1 - core if other else core
    def stored(s):
        to = momentum_out.at[s * CORES + place]
        return pltpu.make_async_copy(momentum.at[s], to, momentum_sem.at[s])

    for s in range(sources):
        stored(s).start()

    def written(k):
        return pltpu.make_async_copy(result.at[k], out.at[(chip ^ k) * CORES + place], sem.at[k])

    def update(k):
        source = chip ^ k
        slot = source * CORES + place
        block = blocks[k]
        parts = block[block.shape[0] - NORM_ROWS :].astype(jnp.float32)
        norm = parts[0:1, 0:1] + parts[1:2, 0:1] + parts[2:3, 0:1]
        unpack(block[: block.shape[0] - NORM_ROWS], matrix.at[k])
        start = (momentum[source] * (1.0 / norm)).astype(jnp.bfloat16)
        step = (QUINTIC_A * QUINTIC_A) * start.astype(jnp.float32) + small_dot(start, matrix[k])
        result[k] = base[slot] - step * (step_size * scales[pl.ds(slot, 1)])

    def only(k, act):
        if sources == chips:
            act()
        else:
            pl.when((chip ^ k) < sources)(act)

    for first in range(0, chips, TOGETHER):
        for k in range(first, first + TOGETHER):
            only(k, functools.partial(update, k))
        for k in range(first, first + TOGETHER):
            only(k, lambda k=k: written(k).start())
    for k in range(chips):
        only(k, lambda k=k: written(k).wait())
    for s in range(sources):
        stored(s).wait()


def weights(base, scales, momentum, blocks, filled=()):
    chips = len(blocks)
    slots, rows, cols = base.shape
    ins = [(VMEM, value) for value in (base, scales, momentum, *blocks)]
    aliases = {len(ins) + i: i for i in range(len(filled))}
    return call(
        functools.partial(weight_kernel, chips, bool(filled), rows * chips * CORES),
        "update_weight",
        ins + [(HBM, value) for value in filled],
        [(HBM, base.shape, jnp.float32)] * 2,
        [
            pltpu.VMEM((chips, cols, cols), jnp.bfloat16),
            pltpu.VMEM((chips, rows, cols), jnp.float32),
            pltpu.SemaphoreType.DMA((chips,)),
            pltpu.SemaphoreType.DMA((slots // CORES,)),
        ],
        aliases=aliases,
    )


def key_kernel(peak, weight, out):
    owner, _, _ = whereabouts()
    heads_own, _, cols = weight.shape
    for i in range(heads_own):
        gamma = head_scale(peak, owner * heads_own + i, (1, cols))
        out[i] = weight[i] * jnp.sqrt(gamma)


def keys(peak, weight):
    (out,) = call(
        key_kernel,
        "scale_keys",
        [(SMEM, peak), (VMEM, weight)],
        [(VMEM, weight.shape, jnp.float32)],
    )
    return out


def body(grad_partials, assignment, momentum, q_weight, k_weight, max_logits):
    heads_own = grad_partials.shape[2]
    sources = lax.axis_size("owner")
    devices = lax.axis_size("dp") * lax.axis_size("context")
    chips = devices // CORES
    assignment = assignment.T

    def swap(value, bits):
        return lax.ppermute(value, PLANE, [(i, i ^ bits) for i in range(devices)])

    g = jnp.transpose(grad_partials[0], (1, 2, 0))
    if (g.shape[2] // chips) % 128:
        g = jnp.transpose(g.reshape(g.shape[:2] + (chips, g.shape[2] // chips)), (0, 2, 1, 3))
    order = list(range(sources))[::-1]
    size = max(1, sources // GROUPS)
    groups = [order[at : at + size] for at in range(0, sources, size)]
    old, first, token = fetch(assignment, g, [[(k, True) for k in groups[0]]], (momentum, max_logits))
    wanted = [[(k, True) for k in order[size:]], [(k, False) for k in groups[0]]]
    others, *own, _ = fetch(assignment, g, wanted, after=[token])
    siblings = [swap(first, 1)]

    near, arrived, before, sent = None, {}, [], []
    first_ks = order[: sources // 2]
    for i, ks in enumerate(groups):
        heads = [(j, j + (size * (i - 1) if i else 0)) for j in range(len(ks))]
        passed = [others] if i == 0 else []
        note = [peak] if i == len(groups) - 2 else []
        values = pair_sums(own[i], siblings[min(i, 1)], heads, chips, before, note, passed)
        here, away = values[0], values[1:chips]
        if i == 0:
            siblings.append(swap(values[chips], 1))
            turned, peak = turn(momentum, swap(old, 1), max_logits)
            wanted = [[(k, False) for k in ks] for ks in groups[1:]]
            *own[1:], _ = fetch(assignment, g, wanted, after=[away[0]])
        away = [swap(value, CORES * (k + 1)) for k, value in enumerate(away)]
        before = away[:2] if i else [away[0], turned]
        totals = list(plane_sums(here, away, [k == 0 for k in ks], sent, note))
        if note:
            peak = totals.pop()
            base, scales = bases(assignment, peak, q_weight, heads_own, k_weight.shape[2])
            k_weight_out = keys(peak, k_weight)
        sent = []
        for k, total in zip(ks, totals):
            if k == 0:
                near = total
            else:
                arrived[k] = lax.ppermute(total, "owner", [(j, j ^ k) for j in range(sources)])
                sent.append(arrived[k])
        if note:
            early = early_grams(assignment, turned, [arrived[k] for k in first_ks], first_ks, heads_own)
            sent += [base, k_weight_out, early[2]]

    arrived = [arrived[k] for k in range(1, sources // 2)]
    new, here, *away = grams(assignment, turned, near, early, arrived, chips, heads_own, [])
    away = [swap(value, CORES * (k + 1)) for k, value in enumerate(away)]
    result = newton(here, away[::-1], momentum.shape[2], [])
    own_new, sibling_new = turn_back(new, [result])

    sibling_new = swap(sibling_new, 1)
    results = [result] + [swap(result, CORES * k) for k in range(1, chips)]
    sibling_results = [swap(value, 1) for value in results]
    filled = weights(base, scales, own_new, results)
    q_weight_out, momentum_out = weights(base, scales, sibling_new, sibling_results, filled)
    return (momentum_out, q_weight_out, k_weight_out)


def solution(mesh):
    rows = P("owner", ("dp", "context"), None)
    return jax.shard_map(
        body,
        mesh=mesh,
        in_specs=(
            P(("dp", "context"), None, "owner", None),
            P(),
            rows,
            rows,
            rows,
            P("context", None),
        ),
        out_specs=(rows, rows, rows),
        check_vma=False,
    )
```

```python
import functools
import math

import jax
import jax.numpy as jnp
from jax import lax
from jax.experimental import pallas as pl
from jax.experimental.pallas import tpu as pltpu
from jax.sharding import PartitionSpec as P

ITERS = 2
MOMENTUM_RATE = 0.95
WEIGHT_KEEP = 0.98
LOGIT_CAP = 100.0
QUINTIC_A = 3.4445
QUINTIC_B = -4.775
QUINTIC_C = 2.0315

CORES = 2
PLANE = ("dp", "context")
NORM_ROWS = 16
TILE = 16
LEVELS = 14.99
STEPS = 8.0
LOWEST = 100.0 * STEPS
NOTE_UNITS = (64.0, 64.0 * 32768.0, 64.0 * 32768.0 * 32768.0)
GROUPS = 4
TOGETHER = 2
LEFT = 128

SMEM = pl.BlockSpec(memory_space=pltpu.SMEM)
VMEM = pl.BlockSpec(memory_space=pltpu.VMEM)
ANY = pl.BlockSpec(memory_space=pl.ANY)
HBM = pl.BlockSpec(memory_space=pltpu.HBM)
PARAMS = pltpu.CompilerParams(vmem_limit_bytes=36 * 1024 * 1024)
FIRST = pltpu.CompilerParams(vmem_limit_bytes=52 * 1024 * 1024)
SECOND = pltpu.CompilerParams(vmem_limit_bytes=44 * 1024 * 1024)


def whereabouts():
    device = lax.axis_index("dp") * lax.axis_size("context") + lax.axis_index("context")
    return lax.axis_index("owner"), device // CORES, device % CORES


def call(kernel, name, ins, outs, scratch=(), after=(), aliases=None, params=PARAMS):
    count = len(ins)

    def whole(*refs):
        kernel(*refs[:count], *refs[count + len(after) :])

    return pl.pallas_call(
        whole,
        in_specs=[spec for spec, _ in ins] + [ANY] * len(after),
        out_specs=[spec for spec, _, _ in outs],
        out_shape=[jax.ShapeDtypeStruct(shape, dtype) for _, shape, dtype in outs],
        scratch_shapes=list(scratch),
        input_output_aliases=aliases or {},
        compiler_params=params,
        name=name,
    )(*[array for _, array in ins], *after)


def head_of(assignment, block, who, place, heads_own):
    found, seen = 0, 0
    for i in range(heads_own):
        hit = (assignment[0, block * heads_own + i] == who).astype(jnp.int32)
        found = jnp.where((hit == 1) & (seen == place), i, found)
        seen = seen + hit
    return found, seen


def bits_of(number):
    rows = jnp.broadcast_to(number.astype(jnp.int32), (TILE, number.shape[1]))
    return lax.shift_right_logical(rows, lax.broadcasted_iota(jnp.int32, rows.shape, 0)) & 1


def number_of(rows):
    bits = rows.astype(jnp.int32) & 1
    bits = lax.shift_left(bits, lax.broadcasted_iota(jnp.int32, bits.shape, 0))
    return jnp.sum(bits.astype(jnp.float32), axis=0, keepdims=True)


def encode(parts, out, note=None):
    top = functools.reduce(jnp.maximum, [jnp.max(jnp.abs(p), axis=0, keepdims=True) for p in parts])
    level = jnp.clip(jnp.ceil(STEPS * jnp.log2(top)), -LOWEST, 128.0 * STEPS)
    factor = jnp.exp2(LEVELS - level * (1.0 / STEPS))
    numbers = [level + LOWEST]
    if note is not None:
        rest = note * NOTE_UNITS[0]
        for _ in NOTE_UNITS:
            numbers.append(jnp.floor(rest))
            rest = (rest - numbers[-1]) * 32768.0
    at = 0
    for p in parts:
        coded = jnp.round(p * factor).astype(jnp.int32)
        if at == 0:
            head = len(numbers) * TILE
            tiles = [
                (coded[i * TILE : (i + 1) * TILE] & -2) | bits_of(number)
                for i, number in enumerate(numbers)
            ]
            for i, tile in enumerate(tiles):
                out[i * TILE : (i + 1) * TILE] = tile.astype(jnp.int16)
            out[head : p.shape[0]] = coded[head:].astype(jnp.int16)
        else:
            out[at : at + p.shape[0]] = coded.astype(jnp.int16)
        at += p.shape[0]


def noted(block, width):
    tiles = [block[i * TILE : (i + 1) * TILE] for i in range(1, 1 + len(NOTE_UNITS))]
    parts = [number_of(tile)[:, :width] / unit for tile, unit in zip(tiles, NOTE_UNITS)]
    return parts[0] + (parts[1] + parts[2])


def decode(block, count):
    size = block.shape[0] // count
    level = number_of(block[:TILE]) - LOWEST
    factor = jnp.exp2(level * (1.0 / STEPS) - LEVELS)
    return [
        block[i * size : (i + 1) * size].astype(jnp.int32).astype(jnp.float32) * factor
        for i in range(count)
    ]


def fetch_kernel(heads_own, wanted, assignment, g, *refs):
    owner, _, core = whereabouts()
    token, outs, sem = refs[-2], refs[:-2], refs[-1]
    if len(refs) > len(wanted) + 2:
        token, outs, sem, held, seen = refs[-4], refs[:-4], *refs[-3:]
    token[...] = jnp.zeros_like(token)
    copies = []
    for group, out in zip(wanted, outs[-len(wanted) :]):
        for i, (k, other) in enumerate(group):
            place = 1 - core if other else core
            head, _ = head_of(assignment, owner, owner ^ k, place, heads_own)
            copies.append(pltpu.make_async_copy(g.at[head], out.at[i], sem.at[len(copies)]))
            copies[-1].start()
    if len(outs) > len(wanted):
        momentum, logits, old = outs[:3]
        cols = momentum.shape[2]
        for s in range(old.shape[0]):
            copies.append(
                pltpu.make_async_copy(momentum.at[s * CORES + 1 - core], held.at[s], sem.at[len(copies)])
            )
            copies[-1].start()
        copies.append(pltpu.make_async_copy(logits, seen, sem.at[len(copies)]))
        copies[-1].start()
    for copy in copies:
        copy.wait()
    if len(outs) > len(wanted):
        old[:, :, :cols] = held[...]
        old[0, 0:1, cols : cols + logits.shape[1]] = seen[...]


def fetch(assignment, g, wanted, rest=(), after=()):
    outs = [(VMEM, (len(group),) + g.shape[1:], g.dtype) for group in wanted]
    count = sum(len(group) for group in wanted)
    ins = [(SMEM, assignment), (ANY, g)]
    outs.append((VMEM, (8, LEFT), jnp.float32))
    held = []
    if rest:
        momentum, logits = rest
        slots, rows, cols = momentum.shape
        outs = [(VMEM, (slots // CORES, rows, 2 * LEFT), momentum.dtype)] + outs
        ins += [(HBM, momentum), (HBM, logits)]
        count += slots // CORES + 1
        held = [
            pltpu.VMEM((slots // CORES, rows, cols), momentum.dtype),
            pltpu.VMEM(logits.shape, logits.dtype),
        ]
    return call(
        functools.partial(fetch_kernel, g.shape[0], wanted),
        "fetch_heads",
        ins,
        outs,
        [pltpu.SemaphoreType.DMA((count,))] + held,
        after,
        params=SECOND if after else FIRST,
    )


def pair_kernel(chips, aligned, heads, passed, own, sibling, *refs):
    _, chip, _ = whereabouts()
    note = None
    refs = refs[passed : len(refs) - passed] if passed else refs
    if len(refs) > chips:
        logits, padded = refs[0], refs[-1]
        padded[...] = jnp.zeros_like(padded)
        padded[:, : logits.shape[1]] = logits[...]
        note, refs = padded[...], refs[1:-1]
    here, away = refs[0], refs[1:]
    width = here.shape[-1]
    for k in range(chips):
        to = chip ^ k
        blocks = []
        for mine, theirs in heads:
            if aligned:
                rows = pl.ds(pl.multiple_of(to * width, 128), width)
                first, second = own[mine, :, rows], sibling[theirs, :, rows]
            else:
                first, second = own[mine, to], sibling[theirs, to]
            blocks.append(first.astype(jnp.float32) + second.astype(jnp.float32))
        if k == 0:
            for i, block in enumerate(blocks):
                here[i] = block
        else:
            encode(blocks, away[k - 1], note if k == 1 else None)


def pair_sums(own, sibling, heads, chips, after, note, passed):
    aligned = own.ndim == 3
    cols = own.shape[-2]
    width = own.shape[-1] // chips if aligned else own.shape[-1]
    coded = (VMEM, (len(heads) * cols, width), jnp.int16)
    outs = [(VMEM, (len(heads), cols, width), jnp.float32)] + [coded] * (chips - 1)
    return call(
        functools.partial(pair_kernel, chips, aligned, heads, len(passed)),
        "pair_sum",
        [(VMEM, own), (VMEM, sibling)]
        + [(ANY, value) for value in passed]
        + [(VMEM, value) for value in note],
        outs + [(ANY, value.shape, value.dtype) for value in passed],
        [pltpu.VMEM((1, width), jnp.float32) for _ in note],
        after=after,
        aliases={2 + i: chips + i for i in range(len(passed))},
    )


def plane_kernel(plain, noting, here, *refs):
    outs = refs[-len(plain) - noting :]
    away = refs[: len(refs) - len(outs)]
    if noting:
        logits, away = away[-1], away[:-1]
        peak, outs = outs[-1], outs[:-1]
        peak[...] = jnp.maximum(logits[...], noted(away[0], logits.shape[1]))
    blocks = [here[i] for i in range(len(plain))]
    for value in away:
        blocks = [a + b for a, b in zip(blocks, decode(value, len(plain)))]
    for is_plain, block, out in zip(plain, blocks, outs):
        if is_plain:
            out[...] = block
        else:
            encode([block], out)


def plane_sums(here, away, plain, after, note):
    _, cols, width = here.shape
    coded = (VMEM, (cols, width), jnp.int16)
    outs = [(VMEM, (cols, width), jnp.float32) if p else coded for p in plain]
    return call(
        functools.partial(plane_kernel, plain, len(note)),
        "plane_sum",
        [(VMEM, value) for value in (here, *away, *note)],
        outs + [(VMEM, value.shape, value.dtype) for value in note],
        after=after,
    )


def turn_kernel(own, sibling, logits, out, peak, both):
    _, _, core = whereabouts()
    rows = own.shape[1]
    for s in range(sibling.shape[0]):
        both[pl.ds(pl.multiple_of(core * rows, 16), rows)] = own[s * CORES + core]
        both[pl.ds(pl.multiple_of((1 - core) * rows, 16), rows)] = sibling[s, :, : own.shape[2]]
        out[s] = both[...].T
    cols = own.shape[2]
    peak[...] = jnp.maximum(logits[...], sibling[0, 0:1, cols : cols + logits.shape[1]])


def turn(own, sibling, logits):
    sources = sibling.shape[0]
    _, rows, cols = own.shape
    return call(
        turn_kernel,
        "turn_momentum",
        [(VMEM, own), (VMEM, sibling), (VMEM, logits)],
        [(VMEM, (sources, cols, CORES * rows), jnp.float32), (VMEM, logits.shape, logits.dtype)],
        [pltpu.VMEM((CORES * rows, cols), jnp.float32)],
    )


def pack(matrix, out):
    cols = matrix.shape[0]
    rest = cols - LEFT
    out[:cols] = matrix[:, :LEFT].astype(out.dtype)
    for f in range(2):
        part = matrix[LEFT + f * rest // 2 : LEFT + (f + 1) * rest // 2, LEFT:]
        out[cols : cols + rest // 2, f * rest : (f + 1) * rest] = part.astype(out.dtype)


def unpack(packed, out):
    cols = out.shape[0]
    rest = cols - LEFT
    out[:, :LEFT] = packed[:cols]
    out[:LEFT, LEFT:] = packed[LEFT:cols].astype(jnp.float32).T.astype(out.dtype)
    for f in range(2):
        part = packed[cols : cols + rest // 2, f * rest : (f + 1) * rest]
        out[LEFT + f * rest // 2 : LEFT + (f + 1) * rest // 2, LEFT:] = part


def refreshed(heads_own, assignment, old, grad, k):
    owner, _, core = whereabouts()
    source = owner ^ k
    _, held = head_of(assignment, source, owner, 0, heads_own)
    kept = old[source]
    return source, jnp.where(held > core, MOMENTUM_RATE * kept + grad, kept)


def gram_of(value, packed, coded):
    value = value.astype(jnp.bfloat16)
    gram = lax.dot_general(
        value, value, (((1,), (1,)), ((), ())), preferred_element_type=jnp.float32
    )
    pack(gram, packed)
    encode([packed[...]], coded)


def early_kernel(heads_own, ks, assignment, old, *refs):
    arrived, (new, packed, coded) = refs[: len(ks)], refs[len(ks) :]
    for i, k in enumerate(ks):
        _, new[i] = refreshed(heads_own, assignment, old, decode(arrived[i], 1)[0], k)
        gram_of(new[i], packed.at[i], coded.at[i])


def early_grams(assignment, old, arrived, ks, heads_own):
    _, cols, width = old.shape
    rows = cols + (cols - LEFT) // 2
    return call(
        functools.partial(early_kernel, heads_own, ks),
        "early_gram",
        [(SMEM, assignment)] + [(VMEM, value) for value in (old, *arrived)],
        [
            (VMEM, (len(ks), cols, width), jnp.float32),
            (VMEM, (len(ks), rows, LEFT), jnp.float32),
            (VMEM, (len(ks), rows, LEFT), jnp.int16),
        ],
    )


def gram_kernel(chips, heads_own, assignment, old, near, early_new, early_packed, early_coded, *refs):
    sources, count = old.shape[0], early_new.shape[0]
    late = sources - count
    arrived, refs = refs[: late - 1], refs[late - 1 :]
    (new, here), away, (packed, coded) = refs[:2], refs[2:-2], refs[-2:]
    owner, chip, _ = whereabouts()
    for k in range(late):
        grad = near[...] if k == 0 else decode(arrived[k - 1], 1)[0]
        source, value = refreshed(heads_own, assignment, old, grad, k)
        new[source] = value
        gram_of(value, packed.at[k], coded.at[k])
    for i in range(count):
        new[owner ^ (sources - 1 - i)] = early_new[i]
    for c in range(chips):
        k = lax.rem(chip ^ c, sources) ^ owner

        def from_early(c=c, k=k):
            if c == 0:
                here[...] = early_packed[sources - 1 - k]
            else:
                away[c - 1][...] = early_coded[sources - 1 - k]

        def from_late(c=c, k=k):
            if c == 0:
                here[...] = packed[k]
            else:
                away[c - 1][...] = coded[k]

        pl.when(k >= late)(from_early)
        pl.when(k < late)(from_late)


def grams(assignment, old, near, early, arrived, chips, heads_own, after):
    sources, cols, _ = old.shape
    rows = cols + (cols - LEFT) // 2
    late = sources - early[0].shape[0]
    coded = (VMEM, (rows, LEFT), jnp.int16)
    return call(
        functools.partial(gram_kernel, chips, heads_own),
        "refresh_and_gram",
        [(SMEM, assignment)] + [(VMEM, value) for value in (old, near, *early, *arrived)],
        [(VMEM, old.shape, jnp.float32), (VMEM, (rows, LEFT), jnp.float32)] + [coded] * (chips - 1),
        [pltpu.VMEM((late, rows, LEFT), jnp.float32), pltpu.VMEM((late, rows, LEFT), jnp.int16)],
        after,
    )


def small_dot(a, b):
    return lax.dot_general(
        a.astype(jnp.bfloat16), b.astype(jnp.bfloat16), (((1,), (0,)), ((), ())),
        preferred_element_type=jnp.float32,
    )


def newton_kernel(here, *refs):
    away, (out, square) = refs[:-2], refs[-2:]
    cols = square.shape[0]
    total = here[...]
    for block in away:
        total = total + decode(block, 1)[0]
    unpack(total, square)
    gram = square[...]
    row = lax.broadcasted_iota(jnp.int32, gram.shape, 0)
    column = lax.broadcasted_iota(jnp.int32, gram.shape, 1)
    square_sum = jnp.sum(jnp.where(row == column, gram, 0.0), axis=(0, 1), keepdims=True)
    norm = jnp.sqrt(square_sum) + 1e-07
    inverse = 1.0 / norm
    gram = jnp.where(norm < jnp.inf, gram * inverse * inverse, 0.0)
    first = QUINTIC_B * gram + QUINTIC_C * small_dot(gram, gram)
    twice = (2.0 * QUINTIC_A) * first + small_dot(first, first)
    gram = (QUINTIC_A * QUINTIC_A) * gram + small_dot(gram, twice)
    second = QUINTIC_B * gram + QUINTIC_C * small_dot(gram, gram)
    result = QUINTIC_A * (first + second) + small_dot(first, second)
    pack(result, out)
    high = norm.astype(jnp.bfloat16).astype(jnp.float32)
    middle = (norm - high).astype(jnp.bfloat16).astype(jnp.float32)
    low = norm - high - middle
    row = lax.broadcasted_iota(jnp.int32, (NORM_ROWS, LEFT), 0)
    scales = jnp.where(row == 0, high, jnp.where(row == 1, middle, jnp.where(row == 2, low, 0.0)))
    out[out.shape[0] - NORM_ROWS :] = scales.astype(jnp.bfloat16)


def newton(here, away, cols, after):
    (out,) = call(
        newton_kernel,
        "newton_schulz",
        [(VMEM, value) for value in (here, *away)],
        [(VMEM, (here.shape[0] + NORM_ROWS, LEFT), jnp.bfloat16)],
        [pltpu.VMEM((cols, cols), jnp.float32)],
        after,
    )
    return out


def back_kernel(new, own, sibling, both):
    _, _, core = whereabouts()
    rows = own.shape[1]
    for s in range(own.shape[0]):
        both[...] = new[s].T
        own[s] = both[pl.ds(pl.multiple_of(core * rows, 16), rows)]
        sibling[s] = both[pl.ds(pl.multiple_of((1 - core) * rows, 16), rows)]


def turn_back(new, after):
    sources, cols, width = new.shape
    half = (VMEM, (sources, width // CORES, cols), jnp.float32)
    return call(
        back_kernel,
        "turn_back",
        [(VMEM, new)],
        [half, half],
        [pltpu.VMEM((width, cols), jnp.float32)],
        after,
    )


def head_scale(peak, head, shape):
    return jnp.minimum(1.0, LOGIT_CAP / jnp.full(shape, peak[0, head], jnp.float32))


def base_kernel(heads_own, kn_count, assignment, peak, weight, out, scales):
    owner, _, _ = whereabouts()
    slots, _, cols = weight.shape
    column = lax.broadcasted_iota(jnp.int32, (1, cols), 1)
    for slot in range(slots):
        source, place = slot // CORES, slot % CORES
        head, held = head_of(assignment, source, owner, place, heads_own)
        gamma = head_scale(peak, source * heads_own + head, (1, cols))
        scale = jnp.where(column < kn_count, jnp.sqrt(gamma), gamma)
        old = weight[slot]
        out[slot] = jnp.where(held > place, (WEIGHT_KEEP * old) * scale, old)
        scales[slot : slot + 1] = jnp.where(held > place, scale, 0.0)


def bases(assignment, peak, weight, heads_own, kn_count):
    slots, _, cols = weight.shape
    return call(
        functools.partial(base_kernel, heads_own, kn_count),
        "scale_weight",
        [(SMEM, assignment), (SMEM, peak), (VMEM, weight)],
        [(VMEM, weight.shape, jnp.float32), (VMEM, (slots, cols), jnp.float32)],
    )


def weight_kernel(chips, other, rows_all, base, scales, momentum, *refs):
    blocks, refs = refs[:chips], refs[chips:]
    out, momentum_out, matrix, result, sem, momentum_sem = refs[-6:]
    slots, _, cols = base.shape
    sources = slots // CORES
    step_size = 0.04 * math.sqrt(max(rows_all, cols))
    _, chip, core = whereabouts()
    place = 1 - core if other else core
    stores = []
    if not other:
        for s in range(sources):
            for half, to in ((momentum, place), (refs[0], 1 - place)):
                to = momentum_out.at[s * CORES + to]
                stores.append(pltpu.make_async_copy(half.at[s], to, momentum_sem.at[len(stores)]))
                stores[-1].start()

    def written(k):
        return pltpu.make_async_copy(result.at[k], out.at[(chip ^ k) * CORES + place], sem.at[k])

    def update(k):
        source = chip ^ k
        slot = source * CORES + place
        block = blocks[k]
        parts = block[block.shape[0] - NORM_ROWS :].astype(jnp.float32)
        norm = parts[0:1, 0:1] + parts[1:2, 0:1] + parts[2:3, 0:1]
        unpack(block[: block.shape[0] - NORM_ROWS], matrix.at[k])
        start = (momentum[source] * (1.0 / norm)).astype(jnp.bfloat16)
        step = (QUINTIC_A * QUINTIC_A) * start.astype(jnp.float32) + small_dot(start, matrix[k])
        result[k] = base[slot] - step * (step_size * scales[pl.ds(slot, 1)])

    def only(k, act):
        if sources == chips:
            act()
        else:
            pl.when((chip ^ k) < sources)(act)

    for first in range(0, chips, TOGETHER):
        for k in range(first, first + TOGETHER):
            only(k, functools.partial(update, k))
        for k in range(first, first + TOGETHER):
            only(k, lambda k=k: written(k).start())
    for k in range(chips):
        only(k, lambda k=k: written(k).wait())
    for store in stores:
        store.wait()


def weights(base, scales, momentum, blocks, sibling=(), filled=()):
    chips = len(blocks)
    slots, rows, cols = base.shape
    ins = [(VMEM, value) for value in (base, scales, momentum, *blocks, *sibling)]
    aliases = {len(ins) + i: i for i in range(len(filled))}
    return call(
        functools.partial(weight_kernel, chips, bool(filled), rows * chips * CORES),
        "update_weight",
        ins + [(HBM, value) for value in filled],
        [(HBM, base.shape, jnp.float32)] * 2,
        [
            pltpu.VMEM((chips, cols, cols), jnp.bfloat16),
            pltpu.VMEM((chips, rows, cols), jnp.float32),
            pltpu.SemaphoreType.DMA((chips,)),
            pltpu.SemaphoreType.DMA((slots,)),
        ],
        aliases=aliases,
    )


def key_kernel(peak, weight, out):
    owner, _, _ = whereabouts()
    heads_own, _, cols = weight.shape
    for i in range(heads_own):
        gamma = head_scale(peak, owner * heads_own + i, (1, cols))
        out[i] = weight[i] * jnp.sqrt(gamma)


def keys(peak, weight):
    (out,) = call(
        key_kernel,
        "scale_keys",
        [(SMEM, peak), (VMEM, weight)],
        [(VMEM, weight.shape, jnp.float32)],
    )
    return out


def body(grad_partials, assignment, momentum, q_weight, k_weight, max_logits):
    heads_own = grad_partials.shape[2]
    sources = lax.axis_size("owner")
    devices = lax.axis_size("dp") * lax.axis_size("context")
    chips = devices // CORES
    assignment = assignment.T

    def swap(value, bits):
        return lax.ppermute(value, PLANE, [(i, i ^ bits) for i in range(devices)])

    g = jnp.transpose(grad_partials[0], (1, 2, 0))
    if (g.shape[2] // chips) % 128:
        g = jnp.transpose(g.reshape(g.shape[:2] + (chips, g.shape[2] // chips)), (0, 2, 1, 3))
    order = list(range(sources))[::-1]
    size = max(1, sources // GROUPS)
    groups = [order[at : at + size] for at in range(0, sources, size)]
    old, first, token = fetch(assignment, g, [[(k, True) for k in groups[0]]], (momentum, max_logits))
    wanted = [[(k, True) for k in order[size:]], [(k, False) for k in groups[0]]]
    others, *own, _ = fetch(assignment, g, wanted, after=[token])
    siblings = [swap(first, 1)]

    near, arrived, before, sent = None, {}, [], []
    first_ks = order[: sources // 2]
    for i, ks in enumerate(groups):
        heads = [(j, j + (size * (i - 1) if i else 0)) for j in range(len(ks))]
        passed = [others] if i == 0 else []
        note = [peak] if i == len(groups) - 2 else []
        values = pair_sums(own[i], siblings[min(i, 1)], heads, chips, before, note, passed)
        here, away = values[0], values[1:chips]
        if i == 0:
            siblings.append(swap(values[chips], 1))
            turned, peak = turn(momentum, swap(old, 1), max_logits)
            wanted = [[(k, False) for k in ks] for ks in groups[1:]]
            *own[1:], _ = fetch(assignment, g, wanted, after=[away[0]])
        away = [swap(value, CORES * (k + 1)) for k, value in enumerate(away)]
        before = away[:2] if i else [away[0], turned]
        totals = list(plane_sums(here, away, [k == 0 for k in ks], sent, note))
        if note:
            peak = totals.pop()
            base, scales = bases(assignment, peak, q_weight, heads_own, k_weight.shape[2])
            k_weight_out = keys(peak, k_weight)
        sent = []
        for k, total in zip(ks, totals):
            if k == 0:
                near = total
            else:
                arrived[k] = lax.ppermute(total, "owner", [(j, j ^ k) for j in range(sources)])
                sent.append(arrived[k])
        if note:
            early = early_grams(assignment, turned, [arrived[k] for k in first_ks], first_ks, heads_own)
            sent += [base, k_weight_out, early[2]]

    arrived = [arrived[k] for k in range(1, sources // 2)]
    new, here, *away = grams(assignment, turned, near, early, arrived, chips, heads_own, [])
    away = [swap(value, CORES * (k + 1)) for k, value in enumerate(away)]
    result = newton(here, away[::-1], momentum.shape[2], [])
    own_new, sibling_new = turn_back(new, [result])

    sibling_new = swap(sibling_new, 1)
    results = [result] + [swap(result, CORES * k) for k in range(1, chips)]
    sibling_results = [swap(value, 1) for value in results]
    filled = weights(base, scales, own_new, results, [sibling_new])
    q_weight_out, momentum_out = weights(base, scales, sibling_new, sibling_results, filled=filled)
    return (momentum_out, q_weight_out, k_weight_out)


def solution(mesh):
    rows = P("owner", ("dp", "context"), None)
    return jax.shard_map(
        body,
        mesh=mesh,
        in_specs=(
            P(("dp", "context"), None, "owner", None),
            P(),
            rows,
            rows,
            rows,
            P("context", None),
        ),
        out_specs=(rows, rows, rows),
        check_vma=False,
    )
```
